32 devices in a mesh: groups: 2 (over x), lon: 16 (over z, y, core).
Axes of the slice: x: 2, y: 2, z: 4, core: 2. Of those that a mesh axis runs over, the one named last changes fastest.
Arguments:
- displacement: float32 [4, 3, 131072], P('groups', None, 'lon'), parts along dimension 0, may hold values from -6 to 6
- s_values: float32 [4], P('groups'), parts along dimension 0, may hold values from 0.2 to 3
- connectivity: int32 [27, 32768], P(None, 'lon'), may hold values from 0 to 8191
- elem_count: int32 [16], P('lon'), may hold values from 512 to 2048, as said below
- shear_modulus: float32 [32768], P('lon'), may hold values from 0.5 to 2
- bulk_modulus: float32 [32768], P('lon'), may hold values from 0.5 to 2
- relax_time: float32 [32768], P('lon'), may hold values from 0.1 to 10
- dev_matrix: float32 [81, 81], replicated, may hold values from -0.5 to 3.5, as said below
- vol_matrix: float32 [81, 81], replicated, may hold values from -0.3 to 2.5, as said below
- left_face: int32 [16, 512], P('lon'), may hold values from 0 to 8191, as said below
- right_face: int32 [16, 512], P('lon'), may hold values from 0 to 8191, as said below
- ice_history: float32 [32768, 256], P('lon'), may hold values from 0 to 2
- ice_send: int32 [16, 128], P('lon'), may hold values from -1 to 2047, as said below
- ice_target: int32 [16, 128], P('lon'), may hold values from -1 to 8191, as said below
Outputs:
- residual: float32 [4, 3, 131072], P('groups', None, 'lon'), parts along dimension 0
The draws below stay inside these ranges and needn't reach their ends.
There are 2 independent parts, one for each index of `groups`. The reference program is written for one: setup_inputs(seed, part) draws one part's arguments, and reference() takes and returns one part's arrays. A program takes and returns all parts, laid end to end along the dimension named above; an argument that names none is the same for every part. Nothing has to cross between parts.
Inputs may be any that keep to these rules, and one draw needn't show every extreme that they name: `elem_count`: some partition has all 2048 slots live. Entries of a row are distinct; a partition's left_face and right_face rows share no node; left_face[p, i] is the same mesh node as right_face[p - 1, i] of partition p - 1 (modulo 16). `right_face`: see left_face. `ice_send`: row q, entries p * 8 to p * 8 + 7: owner q's local ice rows for partition p, filled slots first, -1 in empty ones; some partition gets 8 rows from every owner. `ice_target`: row p, entry q * 8 + c: the node of p that receives the row of ice_send[q, p * 8 + c], -1 exactly where that slot is empty. `dev_matrix`: symmetric. `vol_matrix`: symmetric.
All inputs are finite; a program needn't handle non-finite values.
Results may differ from the reference program's by a relative error of at most 0.0003.
Values sent between devices are 32-bit elements; how exact they have to be, the bound alone decides.
No kernel may reach another device: no remote copies, remote signals or barrier semaphores. Data moves between devices by JAX's collectives and lax.ppermute only.
A program may use at most 192 MiB of HBM per device.

```python
import math
import jax
import jax.numpy as jnp
from jax import lax

PAIR = 2
ELEM_NODES = 27
ELEM_DOF = 81
EPOCHS = 256
ELEM_DEV = 2048
NODE_DEV = 8192
FACE_DEV = 512
ICE_DEV = 2048
CAP = 8
LON_PARTS = 16
SLOTS = 128
NODES = 131072
ELEMS = 32768
ICE_ROWS = 32768
N_LON = 16


def face_nodes(key):
    part_keys = jax.random.split(key, LON_PARTS)
    shuffled = jax.vmap(lambda one_key: jax.random.permutation(one_key, NODE_DEV))(part_keys).astype(jnp.int32)
    return (shuffled[:, :FACE_DEV], shuffled[:, FACE_DEV:2 * FACE_DEV])


def ice_slots(key):
    count_key, busy_key, row_key, node_key = jax.random.split(key, 4)
    counts = jax.random.randint(count_key, (LON_PARTS, LON_PARTS), 0, CAP + 1)
    busiest = jax.random.randint(busy_key, (), 0, LON_PARTS)
    counts = jnp.where(jnp.arange(LON_PARTS)[None, :] == busiest, CAP, counts)
    filled = jnp.arange(CAP)[None, None, :] < counts[:, :, None]
    rows = jax.random.randint(row_key, (LON_PARTS, LON_PARTS, CAP), 0, ICE_DEV)
    nodes = jax.random.randint(node_key, (LON_PARTS, LON_PARTS, CAP), 0, NODE_DEV)
    send_lists = jnp.where(filled, rows, -1).reshape(LON_PARTS, SLOTS)
    target_lists = jnp.where(filled, nodes, -1).transpose(1, 0, 2).reshape(LON_PARTS, SLOTS)
    return (send_lists.astype(jnp.int32), target_lists.astype(jnp.int32))


def element_matrix(key, spread, leading):
    entry_key, diag_key = jax.random.split(key)
    raw = jax.random.uniform(entry_key, (ELEM_DOF, ELEM_DOF), jnp.float32, -spread, spread)
    symmetric = 0.5 * (raw + raw.T)
    diagonal = leading + jax.random.uniform(diag_key, (ELEM_DOF,), jnp.float32, 0.0, 1.0)
    identity = jnp.eye(ELEM_DOF, dtype=bool)
    return jnp.where(identity, diagonal[:, None], symmetric).astype(jnp.float32)


def draw_elem_count(key, part):
    key = jax.random.fold_in(key, 11)
    count_key, full_key = jax.random.split(key)
    counts = jax.random.randint(count_key, (LON_PARTS,), ELEM_DEV // 4, ELEM_DEV + 1)
    fullest = jax.random.randint(full_key, (), 0, LON_PARTS)
    return jnp.where(jnp.arange(LON_PARTS) == fullest, ELEM_DEV, counts).astype(jnp.int32)


def draw_dev_matrix(key, part):
    key = jax.random.fold_in(key, 5)
    return element_matrix(key, 0.5, 2.5)


def draw_vol_matrix(key, part):
    key = jax.random.fold_in(key, 6)
    return element_matrix(key, 0.3, 1.5)


def draw_left_face(key, part):
    western, eastern = face_nodes(key)
    return western


def draw_right_face(key, part):
    western, eastern = face_nodes(key)
    return eastern


def draw_ice_send(key, part):
    send_lists, target_lists = ice_slots(key)
    return send_lists


def draw_ice_target(key, part):
    send_lists, target_lists = ice_slots(key)
    return target_lists


def touch_ends(entries, stream_key, low, largest):
    index_at = [jax.random.randint(jax.random.fold_in(stream_key, axis), (), 0, length) for axis, length in enumerate(entries.shape)]
    widest = entries.shape.index(max(entries.shape))
    neighbour = index_at[:widest] + [(index_at[widest] + 1) % entries.shape[widest]] + index_at[widest + 1:]
    return entries.at[tuple(index_at)].set(low).at[tuple(neighbour)].set(largest)


def levels(key, extent, cuts, least, high):
    loudness, own = 1.0, jax.random.fold_in(key, 6)
    for position, parts in cuts:
        draws = jnp.exp(jax.random.uniform(jax.random.fold_in(own, position), (parts,), jnp.float32, least / len(cuts), high / len(cuts)))
        loudness = loudness * jnp.repeat(draws, extent[position] // parts).reshape([-1 if axis == position else 1 for axis in range(len(extent))])
    return loudness


def gaussian(rng, extent, deviation, bound, cuts=(), kind=jnp.bfloat16):
    entries = deviation * jax.random.normal(rng, extent, jnp.float32)
    if cuts:
        entries = entries * levels(rng, extent, cuts, -0.22, 0.18)
    return jnp.clip(entries, -bound, bound).astype(kind)


def setup_inputs(seed: int = 0, part: int = 0) -> dict:
    key_list = jax.random.split(jax.random.key(seed), 15)
    part_splits = jax.random.split(jax.random.fold_in(key_list[14], part), 15)
    displacement = gaussian(part_splits[0], (PAIR, 3, NODES), 1.0, 6.0, ((2, 16),), jnp.float32)
    s_values = jnp.clip(jnp.exp(jax.random.uniform(part_splits[1], (PAIR,), jnp.float32, math.log(0.2), math.log(3.0))), 0.2, 3.0)
    connectivity = touch_ends(jax.random.randint(key_list[2], (ELEM_NODES, ELEMS), 0, NODE_DEV), jax.random.fold_in(key_list[2], 1), 0, NODE_DEV - 1).astype(jnp.int32)
    elem_count = draw_elem_count(jax.random.fold_in(key_list[14], 71), part)
    shear_modulus = jnp.clip(jnp.exp(math.log(2.0) - 1.3862944 * jax.random.uniform(key_list[4], (ELEMS,), jnp.float32) ** levels(key_list[4], (ELEMS,), ((0, 16),), -0.2, 0.2)), 0.5, 2.0)
    bulk_modulus = jnp.clip(jnp.exp(math.log(2.0) - 1.3862944 * jax.random.uniform(key_list[5], (ELEMS,), jnp.float32) ** levels(key_list[5], (ELEMS,), ((0, 16),), -0.2, 0.2)), 0.5, 2.0)
    relax_time = jnp.clip(jnp.exp(math.log(10.0) - 4.6051702 * jax.random.uniform(key_list[6], (ELEMS,), jnp.float32) ** levels(key_list[6], (ELEMS,), ((0, 16),), -0.2, 0.2)), 0.1, 10.0)
    dev_matrix = draw_dev_matrix(jax.random.fold_in(key_list[14], 71), part)
    vol_matrix = draw_vol_matrix(jax.random.fold_in(key_list[14], 71), part)
    left_face = draw_left_face(jax.random.fold_in(key_list[14], 71), part)
    right_face = draw_right_face(jax.random.fold_in(key_list[14], 71), part)
    ice_history = jnp.clip(2.0 * jax.random.uniform(key_list[11], (ICE_ROWS, EPOCHS), jnp.float32) ** levels(key_list[11], (ICE_ROWS, EPOCHS), ((0, 16),), -0.2, 0.2), 0.0, 2.0)
    ice_send = draw_ice_send(jax.random.fold_in(key_list[14], 71), part)
    ice_target = draw_ice_target(jax.random.fold_in(key_list[14], 71), part)
    return dict(displacement=displacement, s_values=s_values, connectivity=connectivity, elem_count=elem_count, shear_modulus=shear_modulus, bulk_modulus=bulk_modulus, relax_time=relax_time, dev_matrix=dev_matrix, vol_matrix=vol_matrix, left_face=left_face, right_face=right_face, ice_history=ice_history, ice_send=ice_send, ice_target=ice_target)


PRECISE = lax.Precision.HIGHEST


def epoch_weights(s_values, epochs):
    epoch_times = jnp.arange(epochs, dtype=jnp.float32) / epochs
    return jnp.exp(-s_values[:, None] * epoch_times[None, :]) / epochs


def add_to_nodes(values, node_ids, node_total):
    leading = values.shape[:-1]
    flattened = values.reshape(-1, values.shape[-1])
    summed = jax.vmap(lambda one_row: jax.ops.segment_sum(one_row, node_ids, num_segments=node_total))(flattened)
    return summed.reshape(leading + (node_total,))


def element_sums(field_values, s_part, connectivity, live_mask, shear_mod, bulk_mod, relax_span, stacked):
    nodes_per = connectivity.shape[0]
    elem_total = connectivity.shape[1]
    dof_count = stacked.shape[1]
    flat_ids = connectivity.reshape(-1)
    gathered = field_values[:, :, flat_ids].reshape(field_values.shape[0], dof_count, elem_total)
    product = jnp.einsum("ij,sje->sie", stacked, gathered, precision=PRECISE)
    scaled = s_part[:, None] * relax_span[None, :]
    coef_dev = shear_mod[None, :] * (scaled / (scaled + 1.0)) * live_mask[None, :]
    coef_vol = bulk_mod * live_mask
    element = coef_dev[:, None, :] * product[:, :dof_count] + coef_vol[None, None, :] * product[:, dof_count:]
    element = element.reshape(field_values.shape[0], field_values.shape[1], nodes_per * elem_total)
    return add_to_nodes(element, flat_ids, field_values.shape[2])


def radial_force(ice_loads, target, node_total):
    node_ids = jnp.where(target >= 0, target, node_total)
    radial = add_to_nodes(ice_loads, node_ids, node_total)
    zero_part = jnp.zeros_like(radial)
    return jnp.stack([zero_part, zero_part, -radial], axis=1)


def take_faces(sums_one, face_ids):
    return sums_one[:, :, face_ids]


def add_faces(sums_one, left_ids, right_ids, from_prev, from_next):
    return sums_one.at[:, :, left_ids].add(from_prev).at[:, :, right_ids].add(from_next)


def reference(displacement, s_values, connectivity, elem_count, shear_modulus, bulk_modulus, relax_time, dev_matrix, vol_matrix, left_face, right_face, ice_history, ice_send, ice_target):
    part_count = N_LON
    node_dev = displacement.shape[2] // part_count
    elem_dev = connectivity.shape[1] // part_count
    ice_dev = ice_history.shape[0] // part_count
    slot_count = ice_send.shape[1]
    cap_size = slot_count // part_count
    weights = epoch_weights(s_values, ice_history.shape[1])
    offsets = (jnp.arange(part_count, dtype=jnp.int32) * ice_dev)[:, None]
    filled = ice_send >= 0
    rows_global = jnp.where(filled, ice_send + offsets, 0).astype(jnp.int32)
    histories = ice_history[rows_global.reshape(-1)] * filled.reshape(-1, 1).astype(jnp.float32)
    outgoing = jnp.einsum("sk,rk->sr", weights, histories, precision=PRECISE)
    ice_loads = outgoing.reshape(PAIR, part_count, part_count, cap_size).transpose(2, 0, 1, 3).reshape(part_count, PAIR, slot_count)
    field_parts = displacement.reshape(PAIR, 3, part_count, node_dev).transpose(2, 0, 1, 3)
    conn_parts = connectivity.reshape(ELEM_NODES, part_count, elem_dev).transpose(1, 0, 2)
    shear_parts = shear_modulus.reshape(part_count, elem_dev)
    bulk_parts = bulk_modulus.reshape(part_count, elem_dev)
    relax_parts = relax_time.reshape(part_count, elem_dev)
    stacked = jnp.concatenate([dev_matrix, vol_matrix], axis=0)

    def one_part(part_items):
        field_p, conn_p, count_p, shear_p, bulk_p, relax_p, load_p, target_p = part_items
        live_mask = (jnp.arange(elem_dev, dtype=jnp.int32) < count_p).astype(jnp.float32)
        local_sums = element_sums(field_p, s_values, conn_p, live_mask, shear_p, bulk_p, relax_p, stacked)
        return local_sums, radial_force(load_p, target_p, node_dev)

    local_sums, load_force = lax.map(one_part, (field_parts, conn_parts, elem_count, shear_parts, bulk_parts, relax_parts, ice_loads, ice_target))
    from_prev = jax.vmap(take_faces)(jnp.roll(local_sums, 1, axis=0), jnp.roll(right_face, 1, axis=0))
    from_next = jax.vmap(take_faces)(jnp.roll(local_sums, -1, axis=0), jnp.roll(left_face, -1, axis=0))
    assembled = jax.vmap(add_faces)(local_sums, left_face, right_face, from_prev, from_next)
    residual = load_force - assembled
    return residual.transpose(1, 2, 0, 3).reshape(PAIR, 3, part_count * node_dev)
```

```python
import functools

import jax
import jax.numpy as jnp
from jax import lax
from jax.experimental import pallas as pl
from jax.experimental.pallas import tpu as pltpu
from jax.sharding import PartitionSpec as P

F32, BF16, I32 = jnp.float32, jnp.bfloat16, jnp.int32
PRECISE = lax.Precision.HIGHEST
LANES = 128
HI = 256
VMEM = pl.BlockSpec(memory_space=pltpu.VMEM)
SMEM = pl.BlockSpec(memory_space=pltpu.SMEM)


def from_behind(block, axis, distance):
    devices = range(lax.axis_size(axis))
    route = [((i - distance) % len(devices), i) for i in devices]
    return lax.ppermute(block, axis, route)


def epoch_weights(s_values, epochs):
    epoch_times = jnp.arange(epochs, dtype=F32) / epochs
    return jnp.exp(-s_values[:, None] * epoch_times[None, :]) / epochs


def halves(values):
    upper = values.astype(BF16)
    return upper, (values - upper.astype(F32)).astype(BF16)


def node_parts(ids, lo_total):
    width = ids.shape[1]
    hi = jnp.broadcast_to((ids & (HI - 1)).astype(F32), (16, width)).astype(BF16)
    lo = (ids >> 8).astype(F32)
    own = lax.broadcasted_iota(I32, (16, width), 0)
    one, zero = jnp.ones((16, width), BF16), jnp.zeros((16, width), BF16)
    rows = [jnp.where(hi == (own + first).astype(F32).astype(BF16), one, zero) for first in range(0, HI, 16)]
    return jnp.concatenate(rows, axis=0), lo


def read_nodes(table, one_hot, lo, parts_ref, places):
    found = jnp.dot(table, one_hot, preferred_element_type=F32)
    half = found.shape[0] // 2
    found = found[:half] + found[half:]
    lo_total = half // len(places)
    width = lo.shape[1]
    lo8 = jnp.broadcast_to(lo, (8, width))
    own = lax.broadcasted_iota(I32, (8, width), 0).astype(F32)
    masks = [lo8 == own + float(first) for first in range(0, lo_total, 8)]
    for comp, place in enumerate(places):
        chosen = jnp.zeros((8, width), F32)
        for group, mask in enumerate(masks):
            row = comp * lo_total + group * 8
            chosen = jnp.where(mask, found[row : row + 8], chosen)
        for part in range(width // LANES):
            parts_ref[part, pl.ds(place * 8, 8), :] = chosen[:, part * LANES : (part + 1) * LANES]


def finish_reads(parts_ref, part, first, count):
    return sum(parts_ref[part, pl.ds(first * 8 + i, count, stride=8), :] for i in range(8))


def spread(lo, rows, lo_total):
    width = lo.shape[1]
    lo16 = jnp.broadcast_to(lo, (16, width)).astype(BF16)
    own = lax.broadcasted_iota(I32, (16, width), 0).astype(F32)
    masks = [lo16 == (own + float(first)).astype(BF16) for first in range(0, lo_total, 16)]
    zero = jnp.zeros((16, width), BF16)
    blocks = []
    for row in rows:
        if row is None:
            blocks.extend([zero] * len(masks))
            continue
        wide = jnp.broadcast_to(row, (16, width)).astype(BF16)
        blocks.extend(jnp.where(mask, wide, zero) for mask in masks)
    return blocks


def add_nodes(spread_ref, one_hot_ref):
    return lax.dot_general(
        spread_ref[...], one_hot_ref[...], (((1,), (1,)), ((), ())), preferred_element_type=F32
    )


def sums_kernel(
    s_ref, count_ref, disp_ref, conn_ref, shear_ref, bulk_ref, relax_ref, dev_ref, vol_ref, left_ref, right_ref,
    sums_ref, east_ref, west_ref,
    table, matrices, coefs, parts, reads, forces, spreads, one_hots, total,
):
    pair, dims, node_total = disp_ref.shape
    comps = pair * dims
    nodes_per, elem_total = conn_ref.shape
    lo_total = node_total // HI
    dofs = dims * nodes_per
    width = one_hots.shape[1] // nodes_per

    def fill_table(source):
        upper, lower = halves(source)
        table[0 : comps * lo_total] = upper
        table[comps * lo_total :] = lower

    for comp in range(comps):
        for lo in range(lo_total):
            sums_ref[comp * lo_total + lo : comp * lo_total + lo + 1, :] = disp_ref[
                comp // dims, comp % dims : comp % dims + 1, lo * HI : (lo + 1) * HI
            ]
    fill_table(sums_ref[...])

    matrices[...] = jnp.zeros_like(matrices)
    for place, ref in ((0, dev_ref), (1, vol_ref)):
        for half, value in enumerate(halves(ref[...])):
            matrices[half, place, 0:dofs, 0:dofs] = value

    lane_rows = shear_ref.shape[0]
    element = lax.broadcasted_iota(I32, (lane_rows, LANES), 0) * LANES + lax.broadcasted_iota(I32, (lane_rows, LANES), 1)
    live = jnp.where(element < count_ref[0], 1.0, 0.0)
    for one in range(pair):
        scaled = s_ref[one] * relax_ref[...]
        coefs[one] = shear_ref[...] * (scaled / (scaled + 1.0)) * live
    coefs[pair] = bulk_ref[...] * live

    reads[...] = jnp.zeros_like(reads)
    total[...] = jnp.zeros_like(total)
    pad = matrices.shape[2]

    def block(step, carry):
        start = pl.multiple_of(step * width, width)
        for a in range(nodes_per):
            one_hot, lo = node_parts(conn_ref[a : a + 1, pl.ds(start, width)], lo_total)
            one_hots[:, a * width : (a + 1) * width] = one_hot
            read_nodes(table[...], one_hot, lo, parts, [comp * nodes_per + a for comp in range(comps)])
        for one in range(pair):
            for part in range(width // LANES):
                reads[0:dofs, part * LANES : (part + 1) * LANES] = finish_reads(parts, part, one * dofs, dofs)
            upper, lower = halves(reads[...])
            top = matrices[0].reshape(2 * pad, pad)
            low = matrices[1].reshape(2 * pad, pad)
            product = (
                jnp.dot(top, upper, preferred_element_type=F32)
                + jnp.dot(top, lower, preferred_element_type=F32)
                + jnp.dot(low, upper, preferred_element_type=F32)
            )
            row = step * (width // LANES)
            coef_dev = jnp.concatenate([coefs[one, pl.ds(row + i, 1), :] for i in range(width // LANES)], axis=1)
            coef_vol = jnp.concatenate([coefs[pair, pl.ds(row + i, 1), :] for i in range(width // LANES)], axis=1)
            force = coef_dev * product[0:dofs] + coef_vol * product[pad : pad + dofs]
            rounded = force.astype(BF16).astype(F32)
            forces[0, one * dofs : (one + 1) * dofs] = rounded
            forces[1, one * dofs : (one + 1) * dofs] = force - rounded
        for a in range(nodes_per):
            lo = (conn_ref[a : a + 1, pl.ds(start, width)] >> 8).astype(F32)
            rows = [
                forces[half, comp * nodes_per + a : comp * nodes_per + a + 1, :]
                for half in range(2)
                for comp in range(comps)
            ]
            for i, piece in enumerate(spread(lo, rows, lo_total)):
                spreads[i * 16 : (i + 1) * 16, a * width : (a + 1) * width] = piece
        total[...] += add_nodes(spreads, one_hots)
        return carry

    lax.fori_loop(0, elem_total // width, block, 0)

    half = comps * lo_total
    sums = total[0:half] + total[half:]
    sums_ref[...] = sums
    fill_table(sums)
    for face_ref, out_ref in ((right_ref, east_ref), (left_ref, west_ref)):
        for start in range(0, face_ref.shape[1], width):
            one_hot, lo = node_parts(face_ref[:, start : start + width], lo_total)
            read_nodes(table[...], one_hot, lo, parts, list(range(comps)))
            for part in range(width // LANES):
                out_ref[:, start + part * LANES : start + (part + 1) * LANES] = finish_reads(parts, part, 0, comps)


def join_kernel(
    sums_ref, left_ref, right_ref, prev_ref, next_ref, loads_ref, target_ref, out_ref, spreads, one_hots
):
    pair, dims, node_total = out_ref.shape
    comps = pair * dims
    lo_total = node_total // HI
    half = comps * lo_total
    at = 0
    for ids_ref, values_ref in ((left_ref, prev_ref), (right_ref, next_ref), (target_ref, loads_ref)):
        columns = ids_ref.shape[1]
        one_hot, lo = node_parts(ids_ref[...], lo_total)
        one_hots[:, at : at + columns] = one_hot
        rounded = values_ref[...].astype(BF16).astype(F32)
        rows = []
        for value in (rounded, values_ref[...] - rounded):
            if ids_ref is target_ref:
                for one in range(pair):
                    rows += [None] * (dims - 1) + [value[one : one + 1]]
            else:
                rows += [value[comp : comp + 1] for comp in range(comps)]
        for i, piece in enumerate(spread(lo, rows, lo_total)):
            spreads[i * 16 : (i + 1) * 16, at : at + columns] = piece
        at += columns
    added = add_nodes(spreads, one_hots)
    residual = -(sums_ref[...] + added[0:half] + added[half:])
    for comp in range(comps):
        for lo in range(lo_total):
            out_ref[comp // dims, comp % dims : comp % dims + 1, lo * HI : (lo + 1) * HI] = residual[
                comp * lo_total + lo : comp * lo_total + lo + 1, :
            ]


def body(
    displacement,
    s_values,
    connectivity,
    elem_count,
    shear_modulus,
    bulk_modulus,
    relax_time,
    dev_matrix,
    vol_matrix,
    left_face,
    right_face,
    ice_history,
    ice_send,
    ice_target,
):
    pair, dims, node_total = displacement.shape
    nodes_per, elem_total = connectivity.shape
    comps, lo_total = pair * dims, node_total // HI
    half = comps * lo_total
    dofs = dims * nodes_per
    face_total, slots = left_face.shape[1], ice_send.shape[1]
    width = 256

    weights = epoch_weights(s_values, ice_history.shape[1])
    send_rows = ice_send[0]
    filled = send_rows >= 0
    histories = ice_history[jnp.where(filled, send_rows, 0)] * filled[:, None].astype(F32)
    outgoing = jnp.einsum("sk,rk->sr", weights, histories, precision=PRECISE)
    ice_loads = lax.all_to_all(outgoing, "lon", split_axis=1, concat_axis=1, tiled=True)

    face = jax.ShapeDtypeStruct((comps, face_total), F32)
    rows_of = lambda coef: coef.reshape(elem_total // LANES, LANES)
    sums, east, west = pl.pallas_call(
        sums_kernel,
        out_shape=(jax.ShapeDtypeStruct((half, HI), F32), face, face),
        in_specs=[SMEM, SMEM] + [VMEM] * 9,
        out_specs=(VMEM, VMEM, VMEM),
        scratch_shapes=[
            pltpu.VMEM((2 * half, HI), BF16),
            pltpu.VMEM((2, 2, 96, 96), BF16),
            pltpu.VMEM((pair + 1, elem_total // LANES, LANES), F32),
            pltpu.VMEM((width // LANES, comps * nodes_per * 8, LANES), F32),
            pltpu.VMEM((96, width), F32),
            pltpu.VMEM((2, pair * dofs, width), F32),
            pltpu.VMEM((2 * half, nodes_per * width), BF16),
            pltpu.VMEM((HI, nodes_per * width), BF16),
            pltpu.VMEM((2 * half, HI), F32),
        ],
        compiler_params=pltpu.CompilerParams(vmem_limit_bytes=48 * 2**20),
        cost_estimate=pl.CostEstimate(flops=2 * 2 * 2 * half * HI * nodes_per * elem_total, bytes_accessed=2**21, transcendentals=0),
        name="element_sums",
    )(
        s_values, elem_count, displacement, connectivity, rows_of(shear_modulus), rows_of(bulk_modulus),
        rows_of(relax_time), dev_matrix, vol_matrix, left_face, right_face,
    )
    from_prev = from_behind(east, "lon", 1)
    from_next = from_behind(west, "lon", -1)
    columns = 2 * face_total + slots
    return pl.pallas_call(
        join_kernel,
        out_shape=jax.ShapeDtypeStruct(displacement.shape, F32),
        in_specs=[VMEM] * 7,
        out_specs=VMEM,
        scratch_shapes=[pltpu.VMEM((2 * half, columns), BF16), pltpu.VMEM((HI, columns), BF16)],
        compiler_params=pltpu.CompilerParams(vmem_limit_bytes=48 * 2**20),
        name="join_faces",
    )(sums, left_face, right_face, from_prev, from_next, ice_loads, ice_target)


def solution(mesh):
    placed = (
        P("groups", None, "lon"),
        P("groups"),
        P(None, "lon"),
        P("lon"),
        P("lon"),
        P("lon"),
        P("lon"),
        P(),
        P(),
        P("lon", None),
        P("lon", None),
        P("lon", None),
        P("lon", None),
        P("lon", None),
    )
    return jax.shard_map(
        body, mesh=mesh, in_specs=placed, out_specs=P("groups", None, "lon"), check_vma=False
    )
```

```python
import functools

import jax
import jax.numpy as jnp
from jax import lax
from jax.experimental import pallas as pl
from jax.experimental.pallas import tpu as pltpu
from jax.sharding import PartitionSpec as P

F32, BF16, I32 = jnp.float32, jnp.bfloat16, jnp.int32
LANES = 128
HI = 256
VMEM = pl.BlockSpec(memory_space=pltpu.VMEM)
SMEM = pl.BlockSpec(memory_space=pltpu.SMEM)
HBM = pl.BlockSpec(memory_space=pltpu.HBM)


def swap(block, axis, odd):
    count = lax.axis_size(axis)
    step = -1 if odd else 1
    return lax.ppermute(block, axis, [(i, (i + (step if i % 2 == 0 else -step)) % count) for i in range(count)])


def halves(values):
    upper = values.astype(BF16)
    return upper, (values - upper.astype(F32)).astype(BF16)


def node_parts(ids, lo_total):
    width = ids.shape[1]
    hi = jnp.broadcast_to((ids & (HI - 1)).astype(F32), (16, width)).astype(BF16)
    lo = (ids >> 8).astype(F32)
    own = lax.broadcasted_iota(I32, (16, width), 0)
    one, zero = jnp.ones((16, width), BF16), jnp.zeros((16, width), BF16)
    rows = [jnp.where(hi == (own + first).astype(F32).astype(BF16), one, zero) for first in range(0, HI, 16)]
    return jnp.concatenate(rows, axis=0), lo


def read_nodes(table, one_hot, lo, parts_ref, places):
    found = jnp.dot(table, one_hot, preferred_element_type=F32)
    half = found.shape[0] // 2
    found = found[:half] + found[half:]
    lo_total = half // len(places)
    width = lo.shape[1]
    lo8 = jnp.broadcast_to(lo, (8, width))
    own = lax.broadcasted_iota(I32, (8, width), 0).astype(F32)
    masks = [lo8 == own + float(first) for first in range(0, lo_total, 8)]
    for comp, place in enumerate(places):
        chosen = jnp.zeros((8, width), F32)
        for group, mask in enumerate(masks):
            row = comp * lo_total + group * 8
            chosen = jnp.where(mask, found[row : row + 8], chosen)
        for part in range(width // LANES):
            parts_ref[part, pl.ds(place * 8, 8), :] = chosen[:, part * LANES : (part + 1) * LANES]


def finish_reads(parts_ref, part, first, count):
    return sum(parts_ref[part, pl.ds(first * 8 + i, count, stride=8), :] for i in range(8))


def spread(lo, rows, lo_total):
    width = lo.shape[1]
    lo16 = jnp.broadcast_to(lo, (16, width)).astype(BF16)
    own = lax.broadcasted_iota(I32, (16, width), 0).astype(F32)
    masks = [lo16 == (own + float(first)).astype(BF16) for first in range(0, lo_total, 16)]
    zero = jnp.zeros((16, width), BF16)
    blocks = []
    for row in rows:
        if row is None:
            blocks.extend([zero] * len(masks))
            continue
        wide = jnp.broadcast_to(row, (16, width)).astype(BF16)
        blocks.extend(jnp.where(mask, wide, zero) for mask in masks)
    return blocks


def add_nodes(spread_ref, one_hot_ref):
    return lax.dot_general(
        spread_ref[...], one_hot_ref[...], (((1,), (1,)), ((), ())), preferred_element_type=F32
    )


def loads_kernel(s_ref, send_ref, history_ref, out_ref, rows):
    slots, epochs = rows.shape
    owners, pair, cap = out_ref.shape

    def take(slot, carry):
        sent = send_ref[0, slot]
        row = history_ref[pl.ds(jnp.maximum(sent, 0), 1), :]
        rows[pl.ds(slot, 1), :] = jnp.where(sent >= 0, row, 0.0)
        return carry

    lax.fori_loop(0, slots, take, 0, unroll=8)
    times = lax.broadcasted_iota(I32, (8, epochs), 1).astype(F32) / epochs
    own = lax.broadcasted_iota(I32, (8, epochs), 0)
    rates = jnp.zeros((8, epochs), F32)
    for one in range(pair):
        rates = jnp.where(own == one, s_ref[one], rates)
    weights = jnp.exp(-rates * times) / epochs
    loads = lax.dot_general(
        weights, rows[...], (((1,), (1,)), ((), ())), precision=lax.Precision.HIGHEST, preferred_element_type=F32
    )
    for owner in range(owners):
        out_ref[owner] = loads[0:pair, owner * cap : (owner + 1) * cap]


def sums_kernel(
    s_hbm, count_hbm, disp_hbm, conn_hbm, shear_hbm, bulk_hbm, relax_hbm, dev_hbm, vol_hbm, left_hbm, right_hbm, _,
    sums_ref, first_ref, second_ref,
    s_ref, count_ref, disp_ref, conn_ref, shear_ref, bulk_ref, relax_ref, dev_ref, vol_ref, faces,
    arrived, table, matrices, coefs, parts, reads, forces, spreads, one_hots, total,
):
    parity = lax.rem(lax.axis_index("lon"), 2)
    copies = [
        pltpu.make_async_copy(source, target, arrived.at[i])
        for i, (source, target) in enumerate(
            (
                (disp_hbm, disp_ref), (conn_hbm, conn_ref), (dev_hbm, dev_ref), (vol_hbm, vol_ref),
                (shear_hbm, shear_ref), (bulk_hbm, bulk_ref), (relax_hbm, relax_ref), (s_hbm, s_ref),
                (count_hbm, count_ref), (right_hbm, faces.at[parity]), (left_hbm, faces.at[1 - parity]),
            )
        )
    ]
    for copy in copies:
        copy.start()
    dims, pair, node_total = disp_ref.shape
    comps = pair * dims
    nodes_per, elem_total = conn_ref.shape
    lo_total = node_total // HI
    dofs = dims * nodes_per
    width = one_hots.shape[1] // nodes_per
    lane_parts = width // LANES

    def fill_table(source):
        upper, lower = halves(source)
        table[0 : comps * lo_total] = upper
        table[comps * lo_total :] = lower

    total[...] = jnp.zeros_like(total)
    reads[...] = jnp.zeros_like(reads)
    matrices[...] = jnp.zeros_like(matrices)
    copies[0].wait()
    for comp in range(comps):
        for lo in range(lo_total):
            sums_ref[comp * lo_total + lo : comp * lo_total + lo + 1, :] = disp_ref[
                comp // pair, comp % pair : comp % pair + 1, lo * HI : (lo + 1) * HI
            ]
    fill_table(sums_ref[...])
    for copy in copies[1:]:
        copy.wait()

    pad = matrices.shape[1]
    for place, ref in ((0, dev_ref), (pad, vol_ref)):
        for half, value in enumerate(halves(ref[...])):
            matrices[half, 0:dofs, place : place + dofs] = value

    lane_rows = shear_ref.shape[0]
    element = lax.broadcasted_iota(I32, (lane_rows, LANES), 0) * LANES + lax.broadcasted_iota(I32, (lane_rows, LANES), 1)
    live = jnp.where(element < count_ref[0], 1.0, 0.0)
    for one in range(pair):
        scaled = s_ref[one] * relax_ref[...]
        coefs[one] = shear_ref[...] * (scaled / (scaled + 1.0)) * live
    coefs[pair] = bulk_ref[...] * live

    def read_block(step, carry):
        start = pl.multiple_of(step * width, width)
        for a in range(nodes_per):
            one_hot, lo = node_parts(conn_ref[a : a + 1, pl.ds(start, width)], lo_total)
            places = [((comp % pair) * dims + comp // pair) * nodes_per + a for comp in range(comps)]
            read_nodes(table[...], one_hot, lo, parts, places)
        row = step * lane_parts
        coef_vol = jnp.concatenate([coefs[pair, pl.ds(row + i, 1), :] for i in range(lane_parts)], axis=1)
        for one in range(pair):
            coef_dev = jnp.concatenate([coefs[one, pl.ds(row + i, 1), :] for i in range(lane_parts)], axis=1)
            element_disp = jnp.concatenate([finish_reads(parts, i, one * dofs, dofs) for i in range(lane_parts)], axis=1)
            reads[0:dofs] = coef_dev * element_disp
            reads[pad : pad + dofs] = coef_vol * element_disp
            upper, lower = halves(reads[...])
            force = (
                jnp.dot(matrices[0], upper, preferred_element_type=F32)
                + jnp.dot(matrices[0], lower, preferred_element_type=F32)
                + jnp.dot(matrices[1], upper, preferred_element_type=F32)
            )[0:dofs]
            rounded = force.astype(BF16).astype(F32)
            forces[0, step, one * dofs : (one + 1) * dofs] = rounded
            forces[1, step, one * dofs : (one + 1) * dofs] = force - rounded
        return carry

    def add_block(step, carry):
        start = pl.multiple_of(step * width, width)
        for a in range(nodes_per):
            one_hot, lo = node_parts(conn_ref[a : a + 1, pl.ds(start, width)], lo_total)
            one_hots[:, a * width : (a + 1) * width] = one_hot
            rows = []
            for half in range(2):
                for comp in range(comps):
                    place = ((comp % pair) * dims + comp // pair) * nodes_per + a
                    rows.append(forces[half, step, place : place + 1, :])
            for i, piece in enumerate(spread(lo, rows, lo_total)):
                spreads[i * 16 : (i + 1) * 16, a * width : (a + 1) * width] = piece
        total[...] += add_nodes(spreads, one_hots)
        return carry

    lax.fori_loop(0, elem_total // width, read_block, 0)
    lax.fori_loop(0, elem_total // width, add_block, 0)

    half = comps * lo_total
    sums = total[0:half] + total[half:]
    sums_ref[...] = sums
    fill_table(sums)
    for face, out_ref in enumerate((first_ref, second_ref)):
        for start in range(0, faces.shape[2], width):
            columns = min(width, faces.shape[2] - start)
            one_hot, lo = node_parts(faces[face, :, start : start + columns], lo_total)
            read_nodes(table[...], one_hot, lo, parts, list(range(comps)))
            for part in range(columns // LANES):
                out_ref[:, start + part * LANES : start + (part + 1) * LANES] = finish_reads(parts, part, 0, comps)


def join_kernel(
    sums_hbm, left_ref, right_ref, first_hbm, second_hbm, loads_hbm, target_ref, out_ref,
    arrived, sums_ref, from_faces, by_owner, loads, spreads, one_hots,
):
    parity = lax.rem(lax.axis_index("lon"), 2)
    copies = [
        pltpu.make_async_copy(source, target, arrived.at[i])
        for i, (source, target) in enumerate(
            (
                (first_hbm, from_faces.at[1 - parity]), (second_hbm, from_faces.at[parity]),
                (loads_hbm, by_owner), (sums_hbm, sums_ref),
            )
        )
    ]
    for copy in copies:
        copy.start()
    dims, pair, node_total = out_ref.shape
    comps = pair * dims
    lo_total = node_total // HI
    half = comps * lo_total
    los = []
    at = 0
    for ids_ref in (left_ref, right_ref, target_ref):
        columns = ids_ref.shape[1]
        one_hots[:, at : at + columns], lo = node_parts(ids_ref[...], lo_total)
        los.append((at, columns, lo))
        at += columns
    for copy in copies:
        copy.wait()
    owners, _, cap = by_owner.shape
    for owner in range(owners):
        loads[:, owner * cap : (owner + 1) * cap] = by_owner[owner]
    for (at, columns, lo), values in zip(los, (from_faces[0], from_faces[1], loads[...])):
        rounded = values.astype(BF16).astype(F32)
        rows = []
        for value in (rounded, values - rounded):
            count = value.shape[0]
            rows += [None] * (comps - count) + [value[i : i + 1] for i in range(count)]
        for i, piece in enumerate(spread(lo, rows, lo_total)):
            spreads[i * 16 : (i + 1) * 16, at : at + columns] = piece
    added = add_nodes(spreads, one_hots)
    residual = -(sums_ref[...] + added[0:half] + added[half:])
    for comp in range(comps):
        for lo in range(lo_total):
            out_ref[comp // pair, comp % pair : comp % pair + 1, lo * HI : (lo + 1) * HI] = residual[
                comp * lo_total + lo : comp * lo_total + lo + 1, :
            ]


def body(
    displacement,
    s_values,
    connectivity,
    elem_count,
    shear_modulus,
    bulk_modulus,
    relax_time,
    dev_matrix,
    vol_matrix,
    left_face,
    right_face,
    ice_history,
    ice_send,
    ice_target,
):
    pair, dims, node_total = displacement.shape
    nodes_per, elem_total = connectivity.shape
    comps, lo_total = pair * dims, node_total // HI
    half = comps * lo_total
    dofs = dims * nodes_per
    face_total, slots = left_face.shape[1], ice_send.shape[1]
    width = 512

    owners = lax.axis_size("lon")
    outgoing = pl.pallas_call(
        loads_kernel,
        out_shape=jax.ShapeDtypeStruct((owners, pair, slots // owners), F32),
        in_specs=[SMEM, SMEM, VMEM],
        out_specs=VMEM,
        scratch_shapes=[pltpu.VMEM((slots, ice_history.shape[1]), F32)],
        name="ice_loads",
    )(s_values, ice_send, ice_history)
    ice_loads = lax.all_to_all(outgoing, "lon", split_axis=0, concat_axis=0, tiled=True)

    face = jax.ShapeDtypeStruct((comps, face_total), F32)
    rows_of = lambda coef: coef.reshape(elem_total // LANES, LANES)
    inputs = (
        s_values, elem_count, displacement.transpose(1, 0, 2), connectivity, rows_of(shear_modulus),
        rows_of(bulk_modulus), rows_of(relax_time), dev_matrix, vol_matrix, left_face, right_face,
        outgoing,
    )
    blocks = elem_total // width
    pad = 96
    sums, first, second = pl.pallas_call(
        sums_kernel,
        out_shape=(jax.ShapeDtypeStruct((half, HI), F32), face, face),
        in_specs=[HBM] * len(inputs),
        out_specs=(VMEM, VMEM, VMEM),
        scratch_shapes=[
            *[pltpu.SMEM(x.shape, x.dtype) for x in inputs[:2]],
            *[pltpu.VMEM(x.shape, x.dtype) for x in inputs[2:9]],
            pltpu.VMEM((2, *left_face.shape), I32),
            pltpu.SemaphoreType.DMA((11,)),
            pltpu.VMEM((2 * half, HI), BF16),
            pltpu.VMEM((2, pad, 2 * pad), BF16),
            pltpu.VMEM((pair + 1, elem_total // LANES, LANES), F32),
            pltpu.VMEM((width // LANES, comps * nodes_per * 8, LANES), F32),
            pltpu.VMEM((2 * pad, width), F32),
            pltpu.VMEM((2, blocks, pair * dofs, width), F32),
            pltpu.VMEM((2 * half, nodes_per * width), BF16),
            pltpu.VMEM((HI, nodes_per * width), BF16),
            pltpu.VMEM((2 * half, HI), F32),
        ],
        compiler_params=pltpu.CompilerParams(vmem_limit_bytes=60 * 2**20),
        cost_estimate=pl.CostEstimate(
            flops=2 * 2 * 2 * half * HI * nodes_per * elem_total, bytes_accessed=2**20, transcendentals=0
        ),
        name="element_sums",
    )(*inputs)
    first, second, ice_loads = lax.optimization_barrier((first, second, ice_loads))
    from_first = swap(first, "lon", False)
    from_second = swap(second, "lon", True)
    columns = 2 * face_total + slots
    residual = pl.pallas_call(
        join_kernel,
        out_shape=jax.ShapeDtypeStruct((dims, pair, node_total), F32),
        in_specs=[HBM, VMEM, VMEM, HBM, HBM, HBM, VMEM],
        out_specs=VMEM,
        scratch_shapes=[
            pltpu.SemaphoreType.DMA((4,)),
            pltpu.VMEM((half, HI), F32),
            pltpu.VMEM((2, comps, face_total), F32),
            pltpu.VMEM(outgoing.shape, F32),
            pltpu.VMEM((pair, slots), F32),
            pltpu.VMEM((2 * half, columns), BF16),
            pltpu.VMEM((HI, columns), BF16),
        ],
        compiler_params=pltpu.CompilerParams(vmem_limit_bytes=60 * 2**20),
        name="join_faces",
    )(sums, left_face, right_face, from_first, from_second, ice_loads, ice_target)
    return residual.transpose(1, 0, 2)


def solution(mesh):
    placed = (
        P("groups", None, "lon"),
        P("groups"),
        P(None, "lon"),
        P("lon"),
        P("lon"),
        P("lon"),
        P("lon"),
        P(),
        P(),
        P("lon", None),
        P("lon", None),
        P("lon", None),
        P("lon", None),
        P("lon", None),
    )
    return jax.shard_map(
        body, mesh=mesh, in_specs=placed, out_specs=P("groups", None, "lon"), check_vma=False
    )
```

```python
import functools

import jax
import jax.numpy as jnp
from jax import lax
from jax.experimental import pallas as pl
from jax.experimental.pallas import tpu as pltpu
from jax.sharding import PartitionSpec as P

F32, BF16, I32 = jnp.float32, jnp.bfloat16, jnp.int32
LANES = 128
HI = 256
VMEM = pl.BlockSpec(memory_space=pltpu.VMEM)
SMEM = pl.BlockSpec(memory_space=pltpu.SMEM)


def swap(block, axis, odd):
    count = lax.axis_size(axis)
    step = -1 if odd else 1
    return lax.ppermute(block, axis, [(i, (i + (step if i % 2 == 0 else -step)) % count) for i in range(count)])


def halves(values):
    upper = values.astype(BF16)
    return upper, (values - upper.astype(F32)).astype(BF16)


def node_parts(ids, lo_total):
    width = ids.shape[1]
    hi = jnp.broadcast_to((ids & (HI - 1)).astype(F32), (16, width)).astype(BF16)
    lo = (ids >> 8).astype(F32)
    own = lax.broadcasted_iota(I32, (16, width), 0)
    one, zero = jnp.ones((16, width), BF16), jnp.zeros((16, width), BF16)
    rows = [jnp.where(hi == (own + first).astype(F32).astype(BF16), one, zero) for first in range(0, HI, 16)]
    return jnp.concatenate(rows, axis=0), lo


def read_nodes(table, one_hot, lo, parts_ref, places):
    found = jnp.dot(table, one_hot, preferred_element_type=F32)
    half = found.shape[0] // 2
    found = found[:half] + found[half:]
    lo_total = half // len(places)
    width = lo.shape[1]
    lo8 = jnp.broadcast_to(lo, (8, width))
    own = lax.broadcasted_iota(I32, (8, width), 0).astype(F32)
    masks = [lo8 == own + float(first) for first in range(0, lo_total, 8)]
    for comp, place in enumerate(places):
        chosen = jnp.zeros((8, width), F32)
        for group, mask in enumerate(masks):
            row = comp * lo_total + group * 8
            chosen = jnp.where(mask, found[row : row + 8], chosen)
        for part in range(width // LANES):
            parts_ref[part, pl.ds(place * 8, 8), :] = chosen[:, part * LANES : (part + 1) * LANES]


def finish_reads(parts_ref, part, first, count):
    return sum(parts_ref[part, pl.ds(first * 8 + i, count, stride=8), :] for i in range(8))


def spread(lo, rows, lo_total):
    width = lo.shape[1]
    lo16 = jnp.broadcast_to(lo, (16, width)).astype(BF16)
    own = lax.broadcasted_iota(I32, (16, width), 0).astype(F32)
    masks = [lo16 == (own + float(first)).astype(BF16) for first in range(0, lo_total, 16)]
    zero = jnp.zeros((16, width), BF16)
    blocks = []
    for row in rows:
        if row is None:
            blocks.extend([zero] * len(masks))
            continue
        wide = jnp.broadcast_to(row, (16, width)).astype(BF16)
        blocks.extend(jnp.where(mask, wide, zero) for mask in masks)
    return blocks


def add_nodes(spread_ref, one_hot_ref):
    return lax.dot_general(
        spread_ref[...], one_hot_ref[...], (((1,), (1,)), ((), ())), preferred_element_type=F32
    )


def loads_kernel(s_ref, send_ref, history_ref, out_ref, rows):
    slots, epochs = rows.shape
    owners, pair, cap = out_ref.shape

    def take(slot, carry):
        sent = send_ref[0, slot]
        row = history_ref[pl.ds(jnp.maximum(sent, 0), 1), :]
        rows[pl.ds(slot, 1), :] = jnp.where(sent >= 0, row, 0.0)
        return carry

    lax.fori_loop(0, slots, take, 0, unroll=8)
    times = lax.broadcasted_iota(I32, (8, epochs), 1).astype(F32) / epochs
    own = lax.broadcasted_iota(I32, (8, epochs), 0)
    rates = jnp.zeros((8, epochs), F32)
    for one in range(pair):
        rates = jnp.where(own == one, s_ref[:, one : one + 1], rates)
    weights = jnp.exp(-rates * times) / epochs
    upper, lower = halves(weights)
    row_upper, row_lower = halves(rows[...])
    product = lambda a, b: lax.dot_general(a, b, (((1,), (1,)), ((), ())), preferred_element_type=F32)
    loads = product(upper, row_upper) + product(upper, row_lower) + product(lower, row_upper)
    for owner in range(owners):
        out_ref[owner] = loads[0:pair, owner * cap : (owner + 1) * cap]


def sums_kernel(
    s_ref, count_ref, disp_ref, conn_ref, shear_ref, bulk_ref, relax_ref, dev_ref, vol_ref, left_ref, right_ref, _,
    sums_ref, first_ref, second_ref,
    table, matrices, coefs, parts, reads, forces, spreads, one_hots, total,
):
    dims, pair, node_total = disp_ref.shape
    comps = pair * dims
    nodes_per, elem_total = conn_ref.shape
    lo_total = node_total // HI
    dofs = dims * nodes_per
    width = one_hots.shape[1] // nodes_per
    lane_parts = width // LANES

    def fill_table(source):
        upper, lower = halves(source)
        table[0 : comps * lo_total] = upper
        table[comps * lo_total :] = lower

    total[...] = jnp.zeros_like(total)
    reads[...] = jnp.zeros_like(reads)
    matrices[...] = jnp.zeros_like(matrices)
    for comp in range(comps):
        for lo in range(lo_total):
            sums_ref[comp * lo_total + lo : comp * lo_total + lo + 1, :] = disp_ref[
                comp // pair, comp % pair : comp % pair + 1, lo * HI : (lo + 1) * HI
            ]
    fill_table(sums_ref[...])

    pad = matrices.shape[1]
    for place, ref in ((0, dev_ref), (pad, vol_ref)):
        for half, value in enumerate(halves(ref[...])):
            matrices[half, 0:dofs, place : place + dofs] = value

    lane_rows = shear_ref.shape[0]
    element = lax.broadcasted_iota(I32, (lane_rows, LANES), 0) * LANES + lax.broadcasted_iota(I32, (lane_rows, LANES), 1)
    live = jnp.where(element < count_ref[...], 1.0, 0.0)
    for one in range(pair):
        scaled = s_ref[:, one : one + 1] * relax_ref[...]
        coefs[one] = shear_ref[...] * (scaled / (scaled + 1.0)) * live
    coefs[pair] = bulk_ref[...] * live

    def read_block(step, carry):
        start = pl.multiple_of(step * width, width)
        for a in range(nodes_per):
            one_hot, lo = node_parts(conn_ref[a : a + 1, pl.ds(start, width)], lo_total)
            places = [((comp % pair) * dims + comp // pair) * nodes_per + a for comp in range(comps)]
            read_nodes(table[...], one_hot, lo, parts, places)
        row = step * lane_parts
        coef_vol = jnp.concatenate([coefs[pair, pl.ds(row + i, 1), :] for i in range(lane_parts)], axis=1)
        for one in range(pair):
            coef_dev = jnp.concatenate([coefs[one, pl.ds(row + i, 1), :] for i in range(lane_parts)], axis=1)
            element_disp = jnp.concatenate([finish_reads(parts, i, one * dofs, dofs) for i in range(lane_parts)], axis=1)
            reads[0:dofs] = coef_dev * element_disp
            reads[pad : pad + dofs] = coef_vol * element_disp
            upper, lower = halves(reads[...])
            force = (
                jnp.dot(matrices[0], upper, preferred_element_type=F32)
                + jnp.dot(matrices[0], lower, preferred_element_type=F32)
                + jnp.dot(matrices[1], upper, preferred_element_type=F32)
            )[0:dofs]
            rounded = force.astype(BF16).astype(F32)
            forces[0, step, one * dofs : (one + 1) * dofs] = rounded
            forces[1, step, one * dofs : (one + 1) * dofs] = force - rounded
        return carry

    def add_block(step, carry):
        start = pl.multiple_of(step * width, width)
        for a in range(nodes_per):
            one_hot, lo = node_parts(conn_ref[a : a + 1, pl.ds(start, width)], lo_total)
            one_hots[:, a * width : (a + 1) * width] = one_hot
            rows = []
            for half in range(2):
                for comp in range(comps):
                    place = ((comp % pair) * dims + comp // pair) * nodes_per + a
                    rows.append(forces[half, step, place : place + 1, :])
            for i, piece in enumerate(spread(lo, rows, lo_total)):
                spreads[i * 16 : (i + 1) * 16, a * width : (a + 1) * width] = piece
        total[...] += add_nodes(spreads, one_hots)
        return carry

    blocks = jnp.minimum((jnp.max(count_ref[...]) + width - 1) // width, elem_total // width)
    lax.fori_loop(0, blocks, read_block, 0)
    lax.fori_loop(0, blocks, add_block, 0)

    half = comps * lo_total
    sums = total[0:half] + total[half:]
    sums_ref[...] = sums
    fill_table(sums)
    even = lax.rem(lax.axis_index("lon"), 2) == 0
    faces = (jnp.where(even, right_ref[...], left_ref[...]), jnp.where(even, left_ref[...], right_ref[...]))
    for ids, out_ref in zip(faces, (first_ref, second_ref)):
        for start in range(0, ids.shape[1], width):
            columns = min(width, ids.shape[1] - start)
            one_hot, lo = node_parts(ids[:, start : start + columns], lo_total)
            read_nodes(table[...], one_hot, lo, parts, list(range(comps)))
            for part in range(columns // LANES):
                out_ref[:, start + part * LANES : start + (part + 1) * LANES] = finish_reads(parts, part, 0, comps)


def join_kernel(
    sums_ref, left_ref, right_ref, first_ref, second_ref, by_owner, target_ref, out_ref, loads, spreads, one_hots
):
    dims, pair, node_total = out_ref.shape
    comps = pair * dims
    lo_total = node_total // HI
    half = comps * lo_total
    los = []
    at = 0
    for ids_ref in (left_ref, right_ref, target_ref):
        columns = ids_ref.shape[1]
        one_hots[:, at : at + columns], lo = node_parts(ids_ref[...], lo_total)
        los.append((at, columns, lo))
        at += columns
    even = lax.rem(lax.axis_index("lon"), 2) == 0
    from_left = jnp.where(even, second_ref[...], first_ref[...])
    from_right = jnp.where(even, first_ref[...], second_ref[...])
    owners, _, cap = by_owner.shape
    for owner in range(owners):
        loads[:, owner * cap : (owner + 1) * cap] = by_owner[owner]
    for (at, columns, lo), values in zip(los, (from_left, from_right, loads[...])):
        rounded = values.astype(BF16).astype(F32)
        rows = []
        for value in (rounded, values - rounded):
            count = value.shape[0]
            rows += [None] * (comps - count) + [value[i : i + 1] for i in range(count)]
        for i, piece in enumerate(spread(lo, rows, lo_total)):
            spreads[i * 16 : (i + 1) * 16, at : at + columns] = piece
    added = add_nodes(spreads, one_hots)
    residual = -(sums_ref[...] + added[0:half] + added[half:])
    for comp in range(comps):
        for lo in range(lo_total):
            out_ref[comp // pair, comp % pair : comp % pair + 1, lo * HI : (lo + 1) * HI] = residual[
                comp * lo_total + lo : comp * lo_total + lo + 1, :
            ]


def body(
    displacement,
    s_values,
    connectivity,
    elem_count,
    shear_modulus,
    bulk_modulus,
    relax_time,
    dev_matrix,
    vol_matrix,
    left_face,
    right_face,
    ice_history,
    ice_send,
    ice_target,
):
    pair, dims, node_total = displacement.shape
    nodes_per, elem_total = connectivity.shape
    comps, lo_total = pair * dims, node_total // HI
    half = comps * lo_total
    dofs = dims * nodes_per
    face_total, slots = left_face.shape[1], ice_send.shape[1]
    width = 512

    owners = lax.axis_size("lon")
    outgoing = pl.pallas_call(
        loads_kernel,
        out_shape=jax.ShapeDtypeStruct((owners, pair, slots // owners), F32),
        in_specs=[VMEM, SMEM, VMEM],
        out_specs=VMEM,
        scratch_shapes=[pltpu.VMEM((slots, ice_history.shape[1]), F32)],
        name="ice_loads",
    )(s_values.reshape(1, pair), ice_send, ice_history)
    ice_loads = lax.all_to_all(outgoing, "lon", split_axis=0, concat_axis=0, tiled=True)

    face = jax.ShapeDtypeStruct((comps, face_total), F32)
    rows_of = lambda coef: coef.reshape(elem_total // LANES, LANES)
    inputs = (
        s_values.reshape(1, pair), elem_count.reshape(1, 1), displacement.transpose(1, 0, 2), connectivity, rows_of(shear_modulus),
        rows_of(bulk_modulus), rows_of(relax_time), dev_matrix, vol_matrix, left_face, right_face,
        outgoing,
    )
    blocks = elem_total // width
    pad = 96
    sums, first, second = pl.pallas_call(
        sums_kernel,
        out_shape=(jax.ShapeDtypeStruct((half, HI), F32), face, face),
        in_specs=[VMEM] * len(inputs),
        out_specs=(VMEM, VMEM, VMEM),
        scratch_shapes=[
            pltpu.VMEM((2 * half, HI), BF16),
            pltpu.VMEM((2, pad, 2 * pad), BF16),
            pltpu.VMEM((pair + 1, elem_total // LANES, LANES), F32),
            pltpu.VMEM((width // LANES, comps * nodes_per * 8, LANES), F32),
            pltpu.VMEM((2 * pad, width), F32),
            pltpu.VMEM((2, blocks, pair * dofs, width), F32),
            pltpu.VMEM((2 * half, nodes_per * width), BF16),
            pltpu.VMEM((HI, nodes_per * width), BF16),
            pltpu.VMEM((2 * half, HI), F32),
        ],
        compiler_params=pltpu.CompilerParams(vmem_limit_bytes=50 * 2**20),
        cost_estimate=pl.CostEstimate(
            flops=2 * 2 * 2 * half * HI * nodes_per * elem_total, bytes_accessed=2**20, transcendentals=0
        ),
        name="element_sums",
    )(*inputs)
    first, second, ice_loads = lax.optimization_barrier((first, second, ice_loads))
    from_second = swap(second, "lon", True)
    from_first = swap(first, "lon", False)
    columns = 2 * face_total + slots
    residual = pl.pallas_call(
        join_kernel,
        out_shape=jax.ShapeDtypeStruct((dims, pair, node_total), F32),
        in_specs=[VMEM] * 7,
        out_specs=VMEM,
        scratch_shapes=[
            pltpu.VMEM((pair, slots), F32),
            pltpu.VMEM((2 * half, columns), BF16),
            pltpu.VMEM((HI, columns), BF16),
        ],
        compiler_params=pltpu.CompilerParams(vmem_limit_bytes=50 * 2**20),
        name="join_faces",
    )(sums, left_face, right_face, from_first, from_second, ice_loads, ice_target)
    return residual.transpose(1, 0, 2)


def solution(mesh):
    placed = (
        P("groups", None, "lon"),
        P("groups"),
        P(None, "lon"),
        P("lon"),
        P("lon"),
        P("lon"),
        P("lon"),
        P(),
        P(),
        P("lon", None),
        P("lon", None),
        P("lon", None),
        P("lon", None),
        P("lon", None),
    )
    return jax.shard_map(
        body, mesh=mesh, in_specs=placed, out_specs=P("groups", None, "lon"), check_vma=False
    )
```

```python
import functools

import jax
import jax.numpy as jnp
from jax import lax
from jax.experimental import pallas as pl
from jax.experimental.pallas import tpu as pltpu
from jax.sharding import PartitionSpec as P

F32, BF16, I32 = jnp.float32, jnp.bfloat16, jnp.int32
LANES = 128
HI = 256
VMEM = pl.BlockSpec(memory_space=pltpu.VMEM)
ANY = pl.BlockSpec(memory_space=pl.ANY)


def swap(block, axis, odd):
    count = lax.axis_size(axis)
    step = -1 if odd else 1
    return lax.ppermute(block, axis, [(i, (i + (step if i % 2 == 0 else -step)) % count) for i in range(count)])


def halves(values):
    upper = values.astype(BF16)
    return upper, (values - upper.astype(F32)).astype(BF16)


def node_parts(ids, lo_total):
    width = ids.shape[1]
    hi = jnp.broadcast_to((ids & (HI - 1)).astype(F32), (16, width)).astype(BF16)
    lo = (ids >> 8).astype(F32)
    own = lax.broadcasted_iota(I32, (16, width), 0)
    one, zero = jnp.ones((16, width), BF16), jnp.zeros((16, width), BF16)
    rows = [jnp.where(hi == (own + first).astype(F32).astype(BF16), one, zero) for first in range(0, HI, 16)]
    return jnp.concatenate(rows, axis=0), lo


def read_nodes(table, one_hot, lo, parts_ref, places):
    found = jnp.dot(table, one_hot, preferred_element_type=F32)
    half = found.shape[0] // 2
    found = found[:half] + found[half:]
    lo_total = half // len(places)
    width = lo.shape[1]
    lo8 = jnp.broadcast_to(lo, (8, width))
    own = lax.broadcasted_iota(I32, (8, width), 0).astype(F32)
    masks = [lo8 == own + float(first) for first in range(0, lo_total, 8)]
    for comp, place in enumerate(places):
        chosen = jnp.zeros((8, width), F32)
        for group, mask in enumerate(masks):
            row = comp * lo_total + group * 8
            chosen = jnp.where(mask, found[row : row + 8], chosen)
        for part in range(width // LANES):
            parts_ref[part, pl.ds(place * 8, 8), :] = chosen[:, part * LANES : (part + 1) * LANES]


def finish_reads(parts_ref, part, first, count):
    return sum(parts_ref[part, pl.ds(first * 8 + i, count, stride=8), :] for i in range(8))


def spread(lo, rows, lo_total):
    width = lo.shape[1]
    lo16 = jnp.broadcast_to(lo, (16, width)).astype(BF16)
    own = lax.broadcasted_iota(I32, (16, width), 0).astype(F32)
    masks = [lo16 == (own + float(first)).astype(BF16) for first in range(0, lo_total, 16)]
    zero = jnp.zeros((16, width), BF16)
    blocks = []
    for row in rows:
        if row is None:
            blocks.extend([zero] * len(masks))
            continue
        wide = jnp.broadcast_to(row, (16, width)).astype(BF16)
        blocks.extend(jnp.where(mask, wide, zero) for mask in masks)
    return blocks


def add_nodes(spread_ref, one_hot_ref):
    return lax.dot_general(
        spread_ref[...], one_hot_ref[...], (((1,), (1,)), ((), ())), preferred_element_type=F32
    )


def loads_kernel(s_hbm, sent_hbm, history_hbm, out_ref, s_ref, sent_ref, history, by_row, arrived):
    owners, pair, cap = out_ref.shape
    rows, epochs = history.shape
    chunks = 4 if rows % (4 * LANES) == 0 else 1
    chunk = rows // chunks
    copies = [
        pltpu.make_async_copy(
            history_hbm.at[pl.ds(i * chunk, chunk)], history.at[pl.ds(i * chunk, chunk)], arrived.at[i]
        )
        for i in range(chunks)
    ]
    small = [
        pltpu.make_async_copy(s_hbm, s_ref, arrived.at[chunks]),
        pltpu.make_async_copy(sent_hbm, sent_ref, arrived.at[chunks + 1]),
    ]
    for copy in small + copies:
        copy.start()
    for copy in small:
        copy.wait()
    times = lax.broadcasted_iota(I32, (8, epochs), 1).astype(F32) / epochs
    own = lax.broadcasted_iota(I32, (8, epochs), 0)
    rates = jnp.zeros((8, epochs), F32)
    for one in range(pair):
        rates = jnp.where(own == one, s_ref[:, one : one + 1], rates)
    upper, lower = halves(jnp.exp(-rates * times) / epochs)
    both = jnp.concatenate([upper, lower], axis=0)
    product = lambda a, b: lax.dot_general(a, b, (((1,), (1,)), ((), ())), preferred_element_type=F32)
    for i, copy in enumerate(copies):
        copy.wait()
        row_upper, row_lower = halves(history[i * chunk : (i + 1) * chunk, :])
        first = product(both, row_upper)
        by_row[:, i * chunk : (i + 1) * chunk] = first[0:8] + first[8:16] + product(upper, row_lower)
    per = LANES // cap
    for first in range(0, owners * cap, LANES):
        sent = jnp.broadcast_to(sent_ref[:, first : first + LANES], (8, LANES))
        loads = jnp.zeros((8, LANES), F32)
        for at in range(0, rows, LANES):
            found = jnp.take_along_axis(by_row[:, at : at + LANES], sent & (LANES - 1), axis=1, mode="promise_in_bounds")
            loads = jnp.where((sent >= at) & (sent < at + LANES), found, loads)
        for owner in range(per):
            out_ref[first // cap + owner] = loads[0:pair, owner * cap : (owner + 1) * cap]


def sums_kernel(
    s_ref, count_ref, disp_ref, conn_ref, shear_ref, bulk_ref, relax_ref, dev_ref, vol_ref, left_ref, right_ref,
    sums_ref, first_ref, second_ref,
    table, matrices, coefs, parts, reads, forces, spreads, one_hots, total,
):
    dims, pair, node_total = disp_ref.shape
    comps = pair * dims
    nodes_per, elem_total = conn_ref.shape
    lo_total = node_total // HI
    dofs = dims * nodes_per
    width = one_hots.shape[1] // nodes_per
    lane_parts = width // LANES

    def fill_table(source):
        upper, lower = halves(source)
        table[0 : comps * lo_total] = upper
        table[comps * lo_total :] = lower

    total[...] = jnp.zeros_like(total)
    reads[...] = jnp.zeros_like(reads)
    matrices[...] = jnp.zeros_like(matrices)
    for comp in range(comps):
        for lo in range(lo_total):
            sums_ref[comp * lo_total + lo : comp * lo_total + lo + 1, :] = disp_ref[
                comp // pair, comp % pair : comp % pair + 1, lo * HI : (lo + 1) * HI
            ]
    fill_table(sums_ref[...])

    pad = matrices.shape[1]
    for place, ref in ((0, dev_ref), (pad, vol_ref)):
        for half, value in enumerate(halves(ref[...])):
            matrices[half, 0:dofs, place : place + dofs] = value

    lane_rows = shear_ref.shape[0]
    element = lax.broadcasted_iota(I32, (lane_rows, LANES), 0) * LANES + lax.broadcasted_iota(I32, (lane_rows, LANES), 1)
    live = jnp.where(element < count_ref[...], 1.0, 0.0)
    for one in range(pair):
        scaled = s_ref[:, one : one + 1] * relax_ref[...]
        coefs[one] = shear_ref[...] * (scaled / (scaled + 1.0)) * live
    coefs[pair] = bulk_ref[...] * live

    def read_block(step, carry):
        start = pl.multiple_of(step * width, width)
        for a in range(nodes_per):
            one_hot, lo = node_parts(conn_ref[a : a + 1, pl.ds(start, width)], lo_total)
            places = [((comp % pair) * dims + comp // pair) * nodes_per + a for comp in range(comps)]
            read_nodes(table[...], one_hot, lo, parts, places)
        row = step * lane_parts
        coef_vol = jnp.concatenate([coefs[pair, pl.ds(row + i, 1), :] for i in range(lane_parts)], axis=1)
        for one in range(pair):
            coef_dev = jnp.concatenate([coefs[one, pl.ds(row + i, 1), :] for i in range(lane_parts)], axis=1)
            element_disp = jnp.concatenate([finish_reads(parts, i, one * dofs, dofs) for i in range(lane_parts)], axis=1)
            reads[0:dofs] = coef_dev * element_disp
            reads[pad : pad + dofs] = coef_vol * element_disp
            upper, lower = halves(reads[...])
            force = (
                jnp.dot(matrices[0], upper, preferred_element_type=F32)
                + jnp.dot(matrices[0], lower, preferred_element_type=F32)
                + jnp.dot(matrices[1], upper, preferred_element_type=F32)
            )[0:dofs]
            rounded = force.astype(BF16).astype(F32)
            forces[0, step, one * dofs : (one + 1) * dofs] = rounded
            forces[1, step, one * dofs : (one + 1) * dofs] = force - rounded
        return carry

    def add_block(step, carry):
        start = pl.multiple_of(step * width, width)
        for a in range(nodes_per):
            one_hot, lo = node_parts(conn_ref[a : a + 1, pl.ds(start, width)], lo_total)
            one_hots[:, a * width : (a + 1) * width] = one_hot
            rows = []
            for half in range(2):
                for comp in range(comps):
                    place = ((comp % pair) * dims + comp // pair) * nodes_per + a
                    rows.append(forces[half, step, place : place + 1, :])
            for i, piece in enumerate(spread(lo, rows, lo_total)):
                spreads[i * 16 : (i + 1) * 16, a * width : (a + 1) * width] = piece
        total[...] += add_nodes(spreads, one_hots)
        return carry

    blocks = jnp.minimum((jnp.max(count_ref[...]) + width - 1) // width, elem_total // width)
    lax.fori_loop(0, blocks, read_block, 0)
    lax.fori_loop(0, blocks, add_block, 0)

    half = comps * lo_total
    sums = total[0:half] + total[half:]
    sums_ref[...] = sums
    fill_table(sums)
    even = lax.rem(lax.axis_index("lon"), 2) == 0
    faces = (jnp.where(even, right_ref[...], left_ref[...]), jnp.where(even, left_ref[...], right_ref[...]))
    for ids, out_ref in zip(faces, (first_ref, second_ref)):
        for start in range(0, ids.shape[1], width):
            columns = min(width, ids.shape[1] - start)
            one_hot, lo = node_parts(ids[:, start : start + columns], lo_total)
            read_nodes(table[...], one_hot, lo, parts, list(range(comps)))
            for part in range(columns // LANES):
                out_ref[:, start + part * LANES : start + (part + 1) * LANES] = finish_reads(parts, part, 0, comps)


def join_kernel(
    sums_ref, left_ref, right_ref, second_ref, first_ref, by_owner, target_ref, out_ref, loads, spreads, one_hots
):
    dims, pair, node_total = out_ref.shape
    comps = pair * dims
    lo_total = node_total // HI
    half = comps * lo_total
    los = []
    at = 0
    for ids_ref in (left_ref, right_ref, target_ref):
        columns = ids_ref.shape[1]
        one_hots[:, at : at + columns], lo = node_parts(ids_ref[...], lo_total)
        los.append((at, columns, lo))
        at += columns
    even = lax.rem(lax.axis_index("lon"), 2) == 0
    from_left = jnp.where(even, second_ref[...], first_ref[...])
    from_right = jnp.where(even, first_ref[...], second_ref[...])
    owners, _, cap = by_owner.shape
    for owner in range(owners):
        loads[:, owner * cap : (owner + 1) * cap] = by_owner[owner]
    for (at, columns, lo), values in zip(los, (from_left, from_right, loads[...])):
        rounded = values.astype(BF16).astype(F32)
        rows = []
        for value in (rounded, values - rounded):
            count = value.shape[0]
            rows += [None] * (comps - count) + [value[i : i + 1] for i in range(count)]
        for i, piece in enumerate(spread(lo, rows, lo_total)):
            spreads[i * 16 : (i + 1) * 16, at : at + columns] = piece
    added = add_nodes(spreads, one_hots)
    residual = -(sums_ref[...] + added[0:half] + added[half:])
    for comp in range(comps):
        for lo in range(lo_total):
            out_ref[comp // pair, comp % pair : comp % pair + 1, lo * HI : (lo + 1) * HI] = residual[
                comp * lo_total + lo : comp * lo_total + lo + 1, :
            ]


def body(
    displacement,
    s_values,
    connectivity,
    elem_count,
    shear_modulus,
    bulk_modulus,
    relax_time,
    dev_matrix,
    vol_matrix,
    left_face,
    right_face,
    ice_history,
    ice_send,
    ice_target,
):
    pair, dims, node_total = displacement.shape
    nodes_per, elem_total = connectivity.shape
    comps, lo_total = pair * dims, node_total // HI
    half = comps * lo_total
    dofs = dims * nodes_per
    face_total, slots = left_face.shape[1], ice_send.shape[1]
    width = 512

    owners = lax.axis_size("lon")
    outgoing = pl.pallas_call(
        loads_kernel,
        out_shape=jax.ShapeDtypeStruct((owners, pair, slots // owners), F32),
        in_specs=[ANY] * 3,
        out_specs=VMEM,
        scratch_shapes=[
            pltpu.VMEM((1, pair), F32),
            pltpu.VMEM(ice_send.shape, I32),
            pltpu.VMEM(ice_history.shape, F32),
            pltpu.VMEM((8, ice_history.shape[0]), F32),
            pltpu.SemaphoreType.DMA((6,)),
        ],
        name="ice_loads",
    )(s_values.reshape(1, pair), ice_send, ice_history)
    dev_matrix, outgoing = lax.optimization_barrier((dev_matrix, outgoing))
    ice_loads = lax.all_to_all(outgoing, "lon", split_axis=0, concat_axis=0, tiled=True)

    face = jax.ShapeDtypeStruct((comps, face_total), F32)
    rows_of = lambda coef: coef.reshape(elem_total // LANES, LANES)
    inputs = (
        s_values.reshape(1, pair), elem_count.reshape(1, 1), displacement.transpose(1, 0, 2), connectivity,
        rows_of(shear_modulus), rows_of(bulk_modulus), rows_of(relax_time), dev_matrix, vol_matrix, left_face,
        right_face,
    )
    blocks = elem_total // width
    pad = 96
    sums, first, second = pl.pallas_call(
        sums_kernel,
        out_shape=(jax.ShapeDtypeStruct((half, HI), F32), face, face),
        in_specs=[VMEM] * len(inputs),
        out_specs=(VMEM, VMEM, VMEM),
        scratch_shapes=[
            pltpu.VMEM((2 * half, HI), BF16),
            pltpu.VMEM((2, pad, 2 * pad), BF16),
            pltpu.VMEM((pair + 1, elem_total // LANES, LANES), F32),
            pltpu.VMEM((width // LANES, comps * nodes_per * 8, LANES), F32),
            pltpu.VMEM((2 * pad, width), F32),
            pltpu.VMEM((2, blocks, pair * dofs, width), F32),
            pltpu.VMEM((2 * half, nodes_per * width), BF16),
            pltpu.VMEM((HI, nodes_per * width), BF16),
            pltpu.VMEM((2 * half, HI), F32),
        ],
        compiler_params=pltpu.CompilerParams(vmem_limit_bytes=50 * 2**20),
        cost_estimate=pl.CostEstimate(
            flops=2 * 2 * 2 * half * HI * nodes_per * elem_total, bytes_accessed=2**20, transcendentals=0
        ),
        name="element_sums",
    )(*inputs)
    second, first, ice_loads = lax.optimization_barrier((second, first, ice_loads))
    from_second = swap(second, "lon", True)
    from_first = swap(first, "lon", False)
    columns = 2 * face_total + slots
    residual = pl.pallas_call(
        join_kernel,
        out_shape=jax.ShapeDtypeStruct((dims, pair, node_total), F32),
        in_specs=[VMEM] * 7,
        out_specs=VMEM,
        scratch_shapes=[
            pltpu.VMEM((pair, slots), F32),
            pltpu.VMEM((2 * half, columns), BF16),
            pltpu.VMEM((HI, columns), BF16),
        ],
        compiler_params=pltpu.CompilerParams(vmem_limit_bytes=50 * 2**20),
        name="join_faces",
    )(sums, left_face, right_face, from_second, from_first, ice_loads, ice_target)
    return residual.transpose(1, 0, 2)


def solution(mesh):
    placed = (
        P("groups", None, "lon"),
        P("groups"),
        P(None, "lon"),
        P("lon"),
        P("lon"),
        P("lon"),
        P("lon"),
        P(),
        P(),
        P("lon", None),
        P("lon", None),
        P("lon", None),
        P("lon", None),
        P("lon", None),
    )
    return jax.shard_map(
        body, mesh=mesh, in_specs=placed, out_specs=P("groups", None, "lon"), check_vma=False
    )
```

```python
import functools

import jax
import jax.numpy as jnp
from jax import lax
from jax.experimental import pallas as pl
from jax.experimental.pallas import tpu as pltpu
from jax.sharding import PartitionSpec as P

F32, BF16, F8, I32 = jnp.float32, jnp.bfloat16, jnp.float8_e4m3fn, jnp.int32
LANES = 128
HI = 256
WIDE = 2 * HI
TOP = 256.0
VMEM = pl.BlockSpec(memory_space=pltpu.VMEM)
ANY = pl.BlockSpec(memory_space=pl.ANY)


def swap(block, axis, odd):
    count = lax.axis_size(axis)
    step = -1 if odd else 1
    return lax.ppermute(block, axis, [(i, (i + (step if i % 2 == 0 else -step)) % count) for i in range(count)])


def halves(values):
    upper = values.astype(BF16)
    return upper, (values - upper.astype(F32)).astype(BF16)


def thirds(values):
    parts = []
    for _ in range(3):
        parts.append(values.astype(F8))
        values = values - parts[-1].astype(F32)
    return parts


def step_of(largest):
    return jnp.maximum(largest, 1e-30) / TOP


def wide_parts(ids):
    width = ids.shape[1]
    low = (ids & (HI - 1)).astype(F32)
    upper = (ids >> 8) & (WIDE // HI - 1)
    own = lax.broadcasted_iota(I32, (16, width), 0)
    one, zero = jnp.ones((16, width), BF16), jnp.zeros((16, width), BF16)
    rows = []
    for group in range(WIDE // HI):
        hi = jnp.broadcast_to(jnp.where(upper == group, low, -1.0), (16, width)).astype(BF16)
        rows += [jnp.where(hi == (own + first).astype(F32).astype(BF16), one, zero) for first in range(0, HI, 16)]
    return jnp.concatenate(rows, axis=0).astype(F8), (ids >> 9).astype(F32)


def node_parts(ids, lo_total):
    width = ids.shape[1]
    hi = jnp.broadcast_to((ids & (HI - 1)).astype(F32), (16, width)).astype(BF16)
    lo = (ids >> 8).astype(F32)
    own = lax.broadcasted_iota(I32, (16, width), 0)
    one, zero = jnp.ones((16, width), BF16), jnp.zeros((16, width), BF16)
    rows = [jnp.where(hi == (own + first).astype(F32).astype(BF16), one, zero) for first in range(0, HI, 16)]
    return jnp.concatenate(rows, axis=0), lo


def read_nodes(table, pieces, one_hot, lo, parts_ref, places):
    found = jnp.dot(table, one_hot, preferred_element_type=F32)
    size = found.shape[0] // pieces
    found = sum(found[i * size : (i + 1) * size] for i in range(pieces))
    lo_total = size // len(places)
    width = lo.shape[1]
    lo8 = jnp.broadcast_to(lo, (8, width))
    own = lax.broadcasted_iota(I32, (8, width), 0).astype(F32)
    masks = [lo8 == own + float(first) for first in range(0, lo_total, 8)]
    for comp, place in enumerate(places):
        chosen = jnp.zeros((8, width), F32)
        for group, mask in enumerate(masks):
            row = comp * lo_total + group * 8
            chosen = jnp.where(mask, found[row : row + 8], chosen)
        for part in range(width // LANES):
            parts_ref[part, pl.ds(place * 8, 8), :] = chosen[:, part * LANES : (part + 1) * LANES]


def finish_reads(parts_ref, part, first, count):
    return sum(parts_ref[part, pl.ds(first * 8 + i, count, stride=8), :] for i in range(8))


def spread(lo, rows, lo_total):
    width = lo.shape[1]
    lo16 = jnp.broadcast_to(lo, (16, width)).astype(BF16)
    own = lax.broadcasted_iota(I32, (16, width), 0).astype(F32)
    masks = [lo16 == (own + float(first)).astype(BF16) for first in range(0, lo_total, 16)]
    zero = jnp.zeros((16, width), BF16)
    blocks = []
    for row in rows:
        if row is None:
            blocks.extend([zero] * len(masks))
            continue
        wide = jnp.broadcast_to(row, (16, width)).astype(BF16)
        blocks.extend(jnp.where(mask, wide, zero) for mask in masks)
    return blocks


def spread_wide(lo, rows):
    width = lo.shape[1]
    lo16 = jnp.broadcast_to(lo, (16, width)).astype(BF16)
    mask = lo16 == lax.broadcasted_iota(I32, (16, width), 0).astype(F32).astype(BF16)
    zero = jnp.zeros((16, width), BF16)
    blocks = [jnp.where(mask, jnp.broadcast_to(row, (16, width)).astype(BF16), zero) for row in rows]
    return [jnp.concatenate(blocks[i : i + 2], axis=0).astype(F8) for i in range(0, len(blocks), 2)]


def add_nodes(spread_ref, one_hot_ref):
    return lax.dot_general(
        spread_ref[...], one_hot_ref[...], (((1,), (1,)), ((), ())), preferred_element_type=F32
    )


def loads_kernel(s_hbm, sent_hbm, history_hbm, out_ref, s_ref, sent_ref, history, by_row, arrived):
    owners, pair, cap = out_ref.shape
    rows, epochs = history.shape
    chunks = 4 if rows % (4 * LANES) == 0 else 1
    chunk = rows // chunks
    copies = [
        pltpu.make_async_copy(
            history_hbm.at[pl.ds(i * chunk, chunk)], history.at[pl.ds(i * chunk, chunk)], arrived.at[i]
        )
        for i in range(chunks)
    ]
    small = [
        pltpu.make_async_copy(s_hbm, s_ref, arrived.at[chunks]),
        pltpu.make_async_copy(sent_hbm, sent_ref, arrived.at[chunks + 1]),
    ]
    for copy in small + copies:
        copy.start()
    for copy in small:
        copy.wait()
    times = lax.broadcasted_iota(I32, (8, epochs), 1).astype(F32) / epochs
    own = lax.broadcasted_iota(I32, (8, epochs), 0)
    rates = jnp.zeros((8, epochs), F32)
    for one in range(pair):
        rates = jnp.where(own == one, s_ref[:, one : one + 1], rates)
    upper, lower = halves(jnp.exp(-rates * times) / epochs)
    both = jnp.concatenate([upper, lower], axis=0)
    product = lambda a, b: lax.dot_general(a, b, (((1,), (1,)), ((), ())), preferred_element_type=F32)
    for i, copy in enumerate(copies):
        copy.wait()
        row_upper, row_lower = halves(history[i * chunk : (i + 1) * chunk, :])
        first = product(both, row_upper)
        by_row[:, i * chunk : (i + 1) * chunk] = first[0:8] + first[8:16] + product(upper, row_lower)
    per = LANES // cap
    for first in range(0, owners * cap, LANES):
        sent = jnp.broadcast_to(sent_ref[:, first : first + LANES], (8, LANES))
        loads = jnp.zeros((8, LANES), F32)
        for at in range(0, rows, LANES):
            found = jnp.take_along_axis(by_row[:, at : at + LANES], sent & (LANES - 1), axis=1, mode="promise_in_bounds")
            loads = jnp.where((sent >= at) & (sent < at + LANES), found, loads)
        for owner in range(per):
            out_ref[first // cap + owner] = loads[0:pair, owner * cap : (owner + 1) * cap]


def sums_kernel(
    s_ref, count_ref, disp_ref, conn_ref, shear_ref, bulk_ref, relax_ref, dev_ref, vol_ref, left_ref, right_ref,
    sums_ref, first_ref, second_ref,
    grid, wide_table, table, matrices, coefs, parts, reads, forces, pieces, spreads, one_hots, total,
):
    dims, pair, node_total = disp_ref.shape
    comps = pair * dims
    nodes_per, elem_total = conn_ref.shape
    lo_total = node_total // HI
    dofs = dims * nodes_per
    width = one_hots.shape[1] // nodes_per
    lane_parts = width // LANES

    wide_lo = node_total // WIDE
    size = comps * wide_lo

    total[...] = jnp.zeros_like(total)
    reads[...] = jnp.zeros_like(reads)
    matrices[...] = jnp.zeros_like(matrices)
    for comp in range(comps):
        for lo in range(wide_lo):
            grid[comp * wide_lo + lo : comp * wide_lo + lo + 1, :] = disp_ref[
                comp // pair, comp % pair : comp % pair + 1, lo * WIDE : (lo + 1) * WIDE
            ]
    largest = jnp.max(jnp.max(jnp.abs(grid[...]), axis=0, keepdims=True), axis=1, keepdims=True)
    disp_step = step_of(largest)
    for i, third in enumerate(thirds(grid[...] * (1.0 / disp_step))):
        wide_table[i * size : (i + 1) * size] = third

    pad = matrices.shape[1]
    for place, ref in ((0, dev_ref), (pad, vol_ref)):
        for half, value in enumerate(halves(ref[...])):
            matrices[half, 0:dofs, place : place + dofs] = value

    lane_rows = shear_ref.shape[0]
    element = lax.broadcasted_iota(I32, (lane_rows, LANES), 0) * LANES + lax.broadcasted_iota(I32, (lane_rows, LANES), 1)
    live = jnp.where(element < count_ref[...], 1.0, 0.0)
    for one in range(pair):
        scaled = s_ref[:, one : one + 1] * relax_ref[...]
        coefs[one] = shear_ref[...] * (scaled / (scaled + 1.0)) * live * disp_step
    coefs[pair] = bulk_ref[...] * live * disp_step

    def read_block(step, carry):
        start = pl.multiple_of(step * width, width)
        for a in range(nodes_per):
            one_hot, lo = wide_parts(conn_ref[a : a + 1, pl.ds(start, width)])
            places = [((comp % pair) * dims + comp // pair) * nodes_per + a for comp in range(comps)]
            read_nodes(wide_table[...], 3, one_hot, lo, parts, places)
        row = step * lane_parts
        coef_vol = jnp.concatenate([coefs[pair, pl.ds(row + i, 1), :] for i in range(lane_parts)], axis=1)
        for one in range(pair):
            coef_dev = jnp.concatenate([coefs[one, pl.ds(row + i, 1), :] for i in range(lane_parts)], axis=1)
            element_disp = jnp.concatenate([finish_reads(parts, i, one * dofs, dofs) for i in range(lane_parts)], axis=1)
            reads[0:dofs] = coef_dev * element_disp
            reads[pad : pad + dofs] = coef_vol * element_disp
            upper, lower = halves(reads[...])
            force = (
                jnp.dot(matrices[0], upper, preferred_element_type=F32)
                + jnp.dot(matrices[0], lower, preferred_element_type=F32)
                + jnp.dot(matrices[1], upper, preferred_element_type=F32)
            )[0:dofs]
            forces[step, one * dofs : (one + 1) * dofs] = force
            carry = jnp.maximum(carry, jnp.max(jnp.abs(force), axis=0, keepdims=True))
        return carry

    def add_block(step, force_step):
        start = pl.multiple_of(step * width, width)
        for i, third in enumerate(thirds(forces[step] * (1.0 / force_step))):
            pieces[i] = third.astype(F32)
        for a in range(nodes_per):
            one_hot, lo = wide_parts(conn_ref[a : a + 1, pl.ds(start, width)])
            one_hots[:, a * width : (a + 1) * width] = one_hot
            rows = []
            for i in range(3):
                for comp in range(comps):
                    place = ((comp % pair) * dims + comp // pair) * nodes_per + a
                    rows.append(pieces[i, place : place + 1, :])
            for i, piece in enumerate(spread_wide(lo, rows)):
                spreads[i * 32 : (i + 1) * 32, a * width : (a + 1) * width] = piece
        total[...] += add_nodes(spreads, one_hots)
        return force_step

    blocks = jnp.minimum((jnp.max(count_ref[...]) + width - 1) // width, elem_total // width)
    largest = lax.fori_loop(0, blocks, read_block, jnp.zeros((1, width), F32))
    force_step = step_of(jnp.max(largest, axis=1, keepdims=True))
    lax.fori_loop(0, blocks, add_block, force_step)

    grid[...] = (total[0:size] + total[size : 2 * size] + total[2 * size :]) * force_step
    for row in range(size):
        for part in range(WIDE // HI):
            sums_ref[row * (WIDE // HI) + part : row * (WIDE // HI) + part + 1, :] = grid[
                row : row + 1, part * HI : (part + 1) * HI
            ]
    half = comps * lo_total
    table[0:half], table[half:] = halves(sums_ref[...])
    even = lax.rem(lax.axis_index("lon"), 2) == 0
    faces = (jnp.where(even, right_ref[...], left_ref[...]), jnp.where(even, left_ref[...], right_ref[...]))
    for ids, out_ref in zip(faces, (first_ref, second_ref)):
        for start in range(0, ids.shape[1], width):
            columns = min(width, ids.shape[1] - start)
            one_hot, lo = node_parts(ids[:, start : start + columns], lo_total)
            read_nodes(table[...], 2, one_hot, lo, parts, list(range(comps)))
            for part in range(columns // LANES):
                out_ref[:, start + part * LANES : start + (part + 1) * LANES] = finish_reads(parts, part, 0, comps)


def join_kernel(
    sums_ref, left_ref, right_ref, second_ref, first_ref, by_owner, target_ref, out_ref, loads, spreads, one_hots
):
    dims, pair, node_total = out_ref.shape
    comps = pair * dims
    lo_total = node_total // HI
    half = comps * lo_total
    los = []
    at = 0
    for ids_ref in (left_ref, right_ref, target_ref):
        columns = ids_ref.shape[1]
        one_hots[:, at : at + columns], lo = node_parts(ids_ref[...], lo_total)
        los.append((at, columns, lo))
        at += columns
    even = lax.rem(lax.axis_index("lon"), 2) == 0
    from_left = jnp.where(even, second_ref[...], first_ref[...])
    from_right = jnp.where(even, first_ref[...], second_ref[...])
    owners, _, cap = by_owner.shape
    for owner in range(owners):
        loads[:, owner * cap : (owner + 1) * cap] = by_owner[owner]
    for (at, columns, lo), values in zip(los, (from_left, from_right, loads[...])):
        rounded = values.astype(BF16).astype(F32)
        rows = []
        for value in (rounded, values - rounded):
            count = value.shape[0]
            rows += [None] * (comps - count) + [value[i : i + 1] for i in range(count)]
        for i, piece in enumerate(spread(lo, rows, lo_total)):
            spreads[i * 16 : (i + 1) * 16, at : at + columns] = piece
    added = add_nodes(spreads, one_hots)
    residual = -(sums_ref[...] + added[0:half] + added[half:])
    for comp in range(comps):
        for lo in range(lo_total):
            out_ref[comp // pair, comp % pair : comp % pair + 1, lo * HI : (lo + 1) * HI] = residual[
                comp * lo_total + lo : comp * lo_total + lo + 1, :
            ]


def body(
    displacement,
    s_values,
    connectivity,
    elem_count,
    shear_modulus,
    bulk_modulus,
    relax_time,
    dev_matrix,
    vol_matrix,
    left_face,
    right_face,
    ice_history,
    ice_send,
    ice_target,
):
    pair, dims, node_total = displacement.shape
    nodes_per, elem_total = connectivity.shape
    comps, lo_total = pair * dims, node_total // HI
    half = comps * lo_total
    dofs = dims * nodes_per
    face_total, slots = left_face.shape[1], ice_send.shape[1]
    width = 512

    owners = lax.axis_size("lon")
    outgoing = pl.pallas_call(
        loads_kernel,
        out_shape=jax.ShapeDtypeStruct((owners, pair, slots // owners), F32),
        in_specs=[ANY] * 3,
        out_specs=VMEM,
        scratch_shapes=[
            pltpu.VMEM((1, pair), F32),
            pltpu.VMEM(ice_send.shape, I32),
            pltpu.VMEM(ice_history.shape, F32),
            pltpu.VMEM((8, ice_history.shape[0]), F32),
            pltpu.SemaphoreType.DMA((6,)),
        ],
        name="ice_loads",
    )(s_values.reshape(1, pair), ice_send, ice_history)
    dev_matrix, outgoing = lax.optimization_barrier((dev_matrix, outgoing))
    ice_loads = lax.all_to_all(outgoing, "lon", split_axis=0, concat_axis=0, tiled=True)

    face = jax.ShapeDtypeStruct((comps, face_total), F32)
    rows_of = lambda coef: coef.reshape(elem_total // LANES, LANES)
    inputs = (
        s_values.reshape(1, pair), elem_count.reshape(1, 1), displacement.transpose(1, 0, 2), connectivity,
        rows_of(shear_modulus), rows_of(bulk_modulus), rows_of(relax_time), dev_matrix, vol_matrix, left_face,
        right_face,
    )
    blocks = elem_total // width
    pad = 96
    size = half * HI // WIDE
    sums, first, second = pl.pallas_call(
        sums_kernel,
        out_shape=(jax.ShapeDtypeStruct((half, HI), F32), face, face),
        in_specs=[VMEM] * len(inputs),
        out_specs=(VMEM, VMEM, VMEM),
        scratch_shapes=[
            pltpu.VMEM((size, WIDE), F32),
            pltpu.VMEM((3 * size, WIDE), F8),
            pltpu.VMEM((2 * half, HI), BF16),
            pltpu.VMEM((2, pad, 2 * pad), BF16),
            pltpu.VMEM((pair + 1, elem_total // LANES, LANES), F32),
            pltpu.VMEM((width // LANES, comps * nodes_per * 8, LANES), F32),
            pltpu.VMEM((2 * pad, width), F32),
            pltpu.VMEM((blocks, pair * dofs, width), F32),
            pltpu.VMEM((3, pair * dofs, width), F32),
            pltpu.VMEM((3 * size, nodes_per * width), F8),
            pltpu.VMEM((WIDE, nodes_per * width), F8),
            pltpu.VMEM((3 * size, WIDE), F32),
        ],
        compiler_params=pltpu.CompilerParams(vmem_limit_bytes=50 * 2**20),
        cost_estimate=pl.CostEstimate(
            flops=2 * 2 * 2 * half * HI * nodes_per * elem_total, bytes_accessed=2**20, transcendentals=0
        ),
        name="element_sums",
    )(*inputs)
    second, first, ice_loads = lax.optimization_barrier((second, first, ice_loads))
    from_second = swap(second, "lon", True)
    from_first = swap(first, "lon", False)
    columns = 2 * face_total + slots
    residual = pl.pallas_call(
        join_kernel,
        out_shape=jax.ShapeDtypeStruct((dims, pair, node_total), F32),
        in_specs=[VMEM] * 7,
        out_specs=VMEM,
        scratch_shapes=[
            pltpu.VMEM((pair, slots), F32),
            pltpu.VMEM((2 * half, columns), BF16),
            pltpu.VMEM((HI, columns), BF16),
        ],
        compiler_params=pltpu.CompilerParams(vmem_limit_bytes=50 * 2**20),
        name="join_faces",
    )(sums, left_face, right_face, from_second, from_first, ice_loads, ice_target)
    return residual.transpose(1, 0, 2)


def solution(mesh):
    placed = (
        P("groups", None, "lon"),
        P("groups"),
        P(None, "lon"),
        P("lon"),
        P("lon"),
        P("lon"),
        P("lon"),
        P(),
        P(),
        P("lon", None),
        P("lon", None),
        P("lon", None),
        P("lon", None),
        P("lon", None),
    )
    return jax.shard_map(
        body, mesh=mesh, in_specs=placed, out_specs=P("groups", None, "lon"), check_vma=False
    )
```

```python
import functools

import jax
import jax.numpy as jnp
from jax import lax
from jax.experimental import pallas as pl
from jax.experimental.pallas import tpu as pltpu
from jax.sharding import PartitionSpec as P

F32, BF16, F8, I32 = jnp.float32, jnp.bfloat16, jnp.float8_e4m3fn, jnp.int32
LANES = 128
HI = 256
WIDE = 2 * HI
TOP = 256.0
VMEM = pl.BlockSpec(memory_space=pltpu.VMEM)
ANY = pl.BlockSpec(memory_space=pl.ANY)


def swap(block, axis, odd):
    count = lax.axis_size(axis)
    step = -1 if odd else 1
    return lax.ppermute(block, axis, [(i, (i + (step if i % 2 == 0 else -step)) % count) for i in range(count)])


def halves(values):
    upper = values.astype(BF16)
    return upper, (values - upper.astype(F32)).astype(BF16)


def thirds(values):
    parts = []
    for _ in range(3):
        parts.append(values.astype(F8))
        values = values - parts[-1].astype(F32)
    return parts


def step_of(largest):
    return jnp.maximum(largest, 1e-30) / TOP


def wide_parts(ids):
    width = ids.shape[1]
    low = (ids & (HI - 1)).astype(F32)
    upper = (ids >> 8) & (WIDE // HI - 1)
    own = lax.broadcasted_iota(I32, (16, width), 0)
    one, zero = jnp.ones((16, width), BF16), jnp.zeros((16, width), BF16)
    rows = []
    for group in range(WIDE // HI):
        hi = jnp.broadcast_to(jnp.where(upper == group, low, -1.0), (16, width)).astype(BF16)
        rows += [jnp.where(hi == (own + first).astype(F32).astype(BF16), one, zero) for first in range(0, HI, 16)]
    return jnp.concatenate(rows, axis=0).astype(F8), (ids >> 9).astype(F32)


def node_parts(ids, lo_total):
    width = ids.shape[1]
    hi = jnp.broadcast_to((ids & (HI - 1)).astype(F32), (16, width)).astype(BF16)
    lo = (ids >> 8).astype(F32)
    own = lax.broadcasted_iota(I32, (16, width), 0)
    one, zero = jnp.ones((16, width), BF16), jnp.zeros((16, width), BF16)
    rows = [jnp.where(hi == (own + first).astype(F32).astype(BF16), one, zero) for first in range(0, HI, 16)]
    return jnp.concatenate(rows, axis=0), lo


def read_nodes(table, pieces, one_hot, lo, parts_ref, places):
    found = jnp.dot(table, one_hot, preferred_element_type=F32)
    size = found.shape[0] // pieces
    found = sum(found[i * size : (i + 1) * size] for i in range(pieces))
    lo_total = size // len(places)
    width = lo.shape[1]
    lo8 = jnp.broadcast_to(lo, (8, width))
    own = lax.broadcasted_iota(I32, (8, width), 0).astype(F32)
    masks = [lo8 == own + float(first) for first in range(0, lo_total, 8)]
    for comp, place in enumerate(places):
        chosen = jnp.zeros((8, width), F32)
        for group, mask in enumerate(masks):
            row = comp * lo_total + group * 8
            chosen = jnp.where(mask, found[row : row + 8], chosen)
        for part in range(width // LANES):
            parts_ref[part, pl.ds(place * 8, 8), :] = chosen[:, part * LANES : (part + 1) * LANES]


def finish_reads(parts_ref, part, first, count):
    return sum(parts_ref[part, pl.ds(first * 8 + i, count, stride=8), :] for i in range(8))


def spread(lo, rows, lo_total):
    width = lo.shape[1]
    lo16 = jnp.broadcast_to(lo, (16, width)).astype(BF16)
    own = lax.broadcasted_iota(I32, (16, width), 0).astype(F32)
    masks = [lo16 == (own + float(first)).astype(BF16) for first in range(0, lo_total, 16)]
    zero = jnp.zeros((16, width), BF16)
    blocks = []
    for row in rows:
        if row is None:
            blocks.extend([zero] * len(masks))
            continue
        wide = jnp.broadcast_to(row, (16, width)).astype(BF16)
        blocks.extend(jnp.where(mask, wide, zero) for mask in masks)
    return blocks


def spread_wide(lo, rows):
    width = lo.shape[1]
    lo16 = jnp.broadcast_to(lo, (16, width)).astype(BF16)
    mask = lo16 == lax.broadcasted_iota(I32, (16, width), 0).astype(F32).astype(BF16)
    zero = jnp.zeros((16, width), BF16)
    blocks = [jnp.where(mask, jnp.broadcast_to(row, (16, width)).astype(BF16), zero) for row in rows]
    return [jnp.concatenate(blocks[i : i + 2], axis=0).astype(F8) for i in range(0, len(blocks), 2)]


def add_nodes(spread_ref, one_hot_ref):
    return lax.dot_general(
        spread_ref[...], one_hot_ref[...], (((1,), (1,)), ((), ())), preferred_element_type=F32
    )


def loads_kernel(s_hbm, sent_hbm, history_hbm, out_ref, s_ref, sent_ref, history, by_row, arrived):
    owners, pair, cap = out_ref.shape
    rows, epochs = history.shape
    chunks = 4 if rows % (4 * LANES) == 0 else 1
    chunk = rows // chunks
    copies = [
        pltpu.make_async_copy(
            history_hbm.at[pl.ds(i * chunk, chunk)], history.at[pl.ds(i * chunk, chunk)], arrived.at[i]
        )
        for i in range(chunks)
    ]
    small = [
        pltpu.make_async_copy(s_hbm, s_ref, arrived.at[chunks]),
        pltpu.make_async_copy(sent_hbm, sent_ref, arrived.at[chunks + 1]),
    ]
    for copy in small + copies:
        copy.start()
    for copy in small:
        copy.wait()
    times = lax.broadcasted_iota(I32, (8, epochs), 1).astype(F32) / epochs
    own = lax.broadcasted_iota(I32, (8, epochs), 0)
    rates = jnp.zeros((8, epochs), F32)
    for one in range(pair):
        rates = jnp.where(own == one, s_ref[:, one : one + 1], rates)
    upper, lower = halves(jnp.exp(-rates * times) / epochs)
    both = jnp.concatenate([upper, lower], axis=0)
    product = lambda a, b: lax.dot_general(a, b, (((1,), (1,)), ((), ())), preferred_element_type=F32)
    for i, copy in enumerate(copies):
        copy.wait()
        row_upper, row_lower = halves(history[i * chunk : (i + 1) * chunk, :])
        first = product(both, row_upper)
        by_row[:, i * chunk : (i + 1) * chunk] = first[0:8] + first[8:16] + product(upper, row_lower)
    per = LANES // cap
    for first in range(0, owners * cap, LANES):
        sent = jnp.broadcast_to(sent_ref[:, first : first + LANES], (8, LANES))
        loads = jnp.zeros((8, LANES), F32)
        for at in range(0, rows, LANES):
            found = jnp.take_along_axis(by_row[:, at : at + LANES], sent & (LANES - 1), axis=1, mode="promise_in_bounds")
            loads = jnp.where((sent >= at) & (sent < at + LANES), found, loads)
        for owner in range(per):
            out_ref[first // cap + owner] = loads[0:pair, owner * cap : (owner + 1) * cap]


def sums_kernel(
    s_ref, count_ref, disp_ref, conn_ref, shear_ref, bulk_ref, relax_ref, dev_ref, vol_ref, left_ref, right_ref,
    sums_ref, first_ref, second_ref,
    grid, wide_table, table, matrices, coefs, parts, reads, forces, pieces, spreads, one_hots, total,
):
    dims, pair, node_total = disp_ref.shape
    comps = pair * dims
    nodes_per, elem_total = conn_ref.shape
    lo_total = node_total // HI
    dofs = dims * nodes_per
    width = one_hots.shape[1] // nodes_per
    lane_parts = width // LANES

    wide_lo = node_total // WIDE
    size = comps * wide_lo

    total[...] = jnp.zeros_like(total)
    reads[...] = jnp.zeros_like(reads)
    matrices[...] = jnp.zeros_like(matrices)
    for comp in range(comps):
        for lo in range(wide_lo):
            grid[comp * wide_lo + lo : comp * wide_lo + lo + 1, :] = disp_ref[
                comp // pair, comp % pair : comp % pair + 1, lo * WIDE : (lo + 1) * WIDE
            ]
    largest = jnp.max(jnp.max(jnp.abs(grid[...]), axis=0, keepdims=True), axis=1, keepdims=True)
    disp_step = step_of(largest)
    for i, third in enumerate(thirds(grid[...] * (1.0 / disp_step))):
        wide_table[i * size : (i + 1) * size] = third

    pad = matrices.shape[1]
    for place, ref in ((0, dev_ref), (pad, vol_ref)):
        for half, value in enumerate(halves(ref[...])):
            matrices[half, 0:dofs, place : place + dofs] = value

    lane_rows = shear_ref.shape[0]
    element = lax.broadcasted_iota(I32, (lane_rows, LANES), 0) * LANES + lax.broadcasted_iota(I32, (lane_rows, LANES), 1)
    live = jnp.where(element < count_ref[...], 1.0, 0.0)
    for one in range(pair):
        scaled = s_ref[:, one : one + 1] * relax_ref[...]
        coefs[one] = shear_ref[...] * (scaled / (scaled + 1.0)) * live * disp_step
    coefs[pair] = bulk_ref[...] * live * disp_step

    def read_block(step, carry):
        start = pl.multiple_of(step * width, width)
        for a in range(nodes_per):
            one_hot, lo = wide_parts(conn_ref[a : a + 1, pl.ds(start, width)])
            places = [((comp % pair) * dims + comp // pair) * nodes_per + a for comp in range(comps)]
            read_nodes(wide_table[...], 3, one_hot, lo, parts, places)
        row = step * lane_parts
        coef_vol = jnp.concatenate([coefs[pair, pl.ds(row + i, 1), :] for i in range(lane_parts)], axis=1)
        for one in range(pair):
            coef_dev = jnp.concatenate([coefs[one, pl.ds(row + i, 1), :] for i in range(lane_parts)], axis=1)
            element_disp = jnp.concatenate([finish_reads(parts, i, one * dofs, dofs) for i in range(lane_parts)], axis=1)
            reads[0:dofs] = coef_dev * element_disp
            reads[pad : pad + dofs] = coef_vol * element_disp
            upper, lower = halves(reads[...])
            both = jnp.dot(matrices[...].reshape(2 * pad, 2 * pad), upper, preferred_element_type=F32)
            force = (both[0:pad] + both[pad:] + jnp.dot(matrices[0], lower, preferred_element_type=F32))[0:dofs]
            forces[step, one * dofs : (one + 1) * dofs] = force
            carry = jnp.maximum(carry, jnp.max(jnp.abs(force), axis=0, keepdims=True))
        return carry

    def add_block(step, force_step):
        start = pl.multiple_of(step * width, width)
        for i, third in enumerate(thirds(forces[step] * (1.0 / force_step))):
            pieces[i] = third.astype(F32)
        for a in range(nodes_per):
            one_hot, lo = wide_parts(conn_ref[a : a + 1, pl.ds(start, width)])
            one_hots[:, a * width : (a + 1) * width] = one_hot
            rows = []
            for i in range(3):
                for comp in range(comps):
                    place = ((comp % pair) * dims + comp // pair) * nodes_per + a
                    rows.append(pieces[i, place : place + 1, :])
            for i, piece in enumerate(spread_wide(lo, rows)):
                spreads[i * 32 : (i + 1) * 32, a * width : (a + 1) * width] = piece
        total[...] += add_nodes(spreads, one_hots)
        return force_step

    blocks = jnp.minimum((jnp.max(count_ref[...]) + width - 1) // width, elem_total // width)
    largest = lax.fori_loop(0, blocks, read_block, jnp.zeros((1, width), F32))
    force_step = step_of(jnp.max(largest, axis=1, keepdims=True))
    lax.fori_loop(0, blocks, add_block, force_step)

    grid[...] = (total[0:size] + total[size : 2 * size] + total[2 * size :]) * force_step
    for row in range(size):
        for part in range(WIDE // HI):
            sums_ref[row * (WIDE // HI) + part : row * (WIDE // HI) + part + 1, :] = grid[
                row : row + 1, part * HI : (part + 1) * HI
            ]
    half = comps * lo_total
    table[0:half], table[half:] = halves(sums_ref[...])
    even = lax.rem(lax.axis_index("lon"), 2) == 0
    faces = (jnp.where(even, right_ref[...], left_ref[...]), jnp.where(even, left_ref[...], right_ref[...]))
    for ids, out_ref in zip(faces, (first_ref, second_ref)):
        for start in range(0, ids.shape[1], width):
            columns = min(width, ids.shape[1] - start)
            one_hot, lo = node_parts(ids[:, start : start + columns], lo_total)
            read_nodes(table[...], 2, one_hot, lo, parts, list(range(comps)))
            for part in range(columns // LANES):
                out_ref[:, start + part * LANES : start + (part + 1) * LANES] = finish_reads(parts, part, 0, comps)


def join_kernel(
    sums_ref, left_ref, right_ref, second_ref, first_ref, by_owner, target_ref, out_ref, loads, spreads, one_hots
):
    dims, pair, node_total = out_ref.shape
    comps = pair * dims
    lo_total = node_total // HI
    half = comps * lo_total
    los = []
    at = 0
    for ids_ref in (left_ref, right_ref, target_ref):
        columns = ids_ref.shape[1]
        one_hots[:, at : at + columns], lo = node_parts(ids_ref[...], lo_total)
        los.append((at, columns, lo))
        at += columns
    even = lax.rem(lax.axis_index("lon"), 2) == 0
    from_left = jnp.where(even, second_ref[...], first_ref[...])
    from_right = jnp.where(even, first_ref[...], second_ref[...])
    owners, _, cap = by_owner.shape
    for owner in range(owners):
        loads[:, owner * cap : (owner + 1) * cap] = by_owner[owner]
    for (at, columns, lo), values in zip(los, (from_left, from_right, loads[...])):
        rounded = values.astype(BF16).astype(F32)
        rows = []
        for value in (rounded, values - rounded):
            count = value.shape[0]
            rows += [None] * (comps - count) + [value[i : i + 1] for i in range(count)]
        for i, piece in enumerate(spread(lo, rows, lo_total)):
            spreads[i * 16 : (i + 1) * 16, at : at + columns] = piece
    added = add_nodes(spreads, one_hots)
    residual = -(sums_ref[...] + added[0:half] + added[half:])
    for comp in range(comps):
        for lo in range(lo_total):
            out_ref[comp // pair, comp % pair : comp % pair + 1, lo * HI : (lo + 1) * HI] = residual[
                comp * lo_total + lo : comp * lo_total + lo + 1, :
            ]


def body(
    displacement,
    s_values,
    connectivity,
    elem_count,
    shear_modulus,
    bulk_modulus,
    relax_time,
    dev_matrix,
    vol_matrix,
    left_face,
    right_face,
    ice_history,
    ice_send,
    ice_target,
):
    pair, dims, node_total = displacement.shape
    nodes_per, elem_total = connectivity.shape
    comps, lo_total = pair * dims, node_total // HI
    half = comps * lo_total
    dofs = dims * nodes_per
    face_total, slots = left_face.shape[1], ice_send.shape[1]
    width = 512

    owners = lax.axis_size("lon")
    outgoing = pl.pallas_call(
        loads_kernel,
        out_shape=jax.ShapeDtypeStruct((owners, pair, slots // owners), F32),
        in_specs=[ANY] * 3,
        out_specs=VMEM,
        scratch_shapes=[
            pltpu.VMEM((1, pair), F32),
            pltpu.VMEM(ice_send.shape, I32),
            pltpu.VMEM(ice_history.shape, F32),
            pltpu.VMEM((8, ice_history.shape[0]), F32),
            pltpu.SemaphoreType.DMA((6,)),
        ],
        name="ice_loads",
    )(s_values.reshape(1, pair), ice_send, ice_history)
    dev_matrix, outgoing = lax.optimization_barrier((dev_matrix, outgoing))
    ice_loads = lax.all_to_all(outgoing, "lon", split_axis=0, concat_axis=0, tiled=True)

    face = jax.ShapeDtypeStruct((comps, face_total), F32)
    rows_of = lambda coef: coef.reshape(elem_total // LANES, LANES)
    inputs = (
        s_values.reshape(1, pair), elem_count.reshape(1, 1), displacement.transpose(1, 0, 2), connectivity,
        rows_of(shear_modulus), rows_of(bulk_modulus), rows_of(relax_time), dev_matrix, vol_matrix, left_face,
        right_face,
    )
    blocks = elem_total // width
    pad = 96
    size = half * HI // WIDE
    sums, first, second = pl.pallas_call(
        sums_kernel,
        out_shape=(jax.ShapeDtypeStruct((half, HI), F32), face, face),
        in_specs=[VMEM] * len(inputs),
        out_specs=(VMEM, VMEM, VMEM),
        scratch_shapes=[
            pltpu.VMEM((size, WIDE), F32),
            pltpu.VMEM((3 * size, WIDE), F8),
            pltpu.VMEM((2 * half, HI), BF16),
            pltpu.VMEM((2, pad, 2 * pad), BF16),
            pltpu.VMEM((pair + 1, elem_total // LANES, LANES), F32),
            pltpu.VMEM((width // LANES, comps * nodes_per * 8, LANES), F32),
            pltpu.VMEM((2 * pad, width), F32),
            pltpu.VMEM((blocks, pair * dofs, width), F32),
            pltpu.VMEM((3, pair * dofs, width), F32),
            pltpu.VMEM((3 * size, nodes_per * width), F8),
            pltpu.VMEM((WIDE, nodes_per * width), F8),
            pltpu.VMEM((3 * size, WIDE), F32),
        ],
        compiler_params=pltpu.CompilerParams(vmem_limit_bytes=50 * 2**20),
        cost_estimate=pl.CostEstimate(
            flops=2 * 2 * 2 * half * HI * nodes_per * elem_total, bytes_accessed=2**20, transcendentals=0
        ),
        name="element_sums",
    )(*inputs)
    second, first, ice_loads = lax.optimization_barrier((second, first, ice_loads))
    from_second = swap(second, "lon", True)
    from_first = swap(first, "lon", False)
    columns = 2 * face_total + slots
    residual = pl.pallas_call(
        join_kernel,
        out_shape=jax.ShapeDtypeStruct((dims, pair, node_total), F32),
        in_specs=[VMEM] * 7,
        out_specs=VMEM,
        scratch_shapes=[
            pltpu.VMEM((pair, slots), F32),
            pltpu.VMEM((2 * half, columns), BF16),
            pltpu.VMEM((HI, columns), BF16),
        ],
        compiler_params=pltpu.CompilerParams(vmem_limit_bytes=50 * 2**20),
        name="join_faces",
    )(sums, left_face, right_face, from_second, from_first, ice_loads, ice_target)
    return residual.transpose(1, 0, 2)


def solution(mesh):
    placed = (
        P("groups", None, "lon"),
        P("groups"),
        P(None, "lon"),
        P("lon"),
        P("lon"),
        P("lon"),
        P("lon"),
        P(),
        P(),
        P("lon", None),
        P("lon", None),
        P("lon", None),
        P("lon", None),
        P("lon", None),
    )
    return jax.shard_map(
        body, mesh=mesh, in_specs=placed, out_specs=P("groups", None, "lon"), check_vma=False
    )
```
